256 devices in a mesh: ctx: 64 (over z, y, core), head: 4 (over x).
Axes of the slice: x: 4, y: 4, z: 8, core: 2. Of those that a mesh axis runs over, the one named last changes fastest.
Arguments:
- hidden_in: bfloat16 [32768, 3584], P('ctx', 'head'), may hold values from -60 to 60, as said below
- w_query: bfloat16 [3584, 2048], P(None, 'head'), may hold values from -0.09375 to 0.09375
- w_key: bfloat16 [3584, 512], P(None, 'head'), may hold values from -0.09375 to 0.09375
- w_value: bfloat16 [3584, 512], P(None, 'head'), may hold values from -0.09375 to 0.09375
- w_output: bfloat16 [2048, 3584], P('head'), may hold values from -0.125 to 0.125
- vertical: int32 [4, 4, 4], P('head'), may hold values from 0 to 255
- slash_offsets: int32 [4, 4, 4], P('head'), may hold values from 1 to 255
Outputs:
- attn_out: bfloat16 [32768, 3584], P(('ctx', 'head'))
The draws below stay inside these ranges and needn't reach their ends.
Inputs may be any that keep to these rules, and one draw needn't show every extreme that they name: `hidden_in`: hidden states of order one, with some rows far larger in some draws.
All inputs are finite; a program needn't handle non-finite values.
Results may differ from the reference program's by a relative error of at most 0.012.
The reference program's roundings to bfloat16 on the way (of `weights` and `context`) count: a program that leaves them out, or rounds other values in their place, can miss the bound.
Values may be sent and summed in bfloat16 or wider, within the bound.
No kernel may reach another device: no remote copies, remote signals or barrier semaphores. Data moves between devices by JAX's collectives and lax.ppermute only.
A program may use at most 128 MiB of HBM per device.

```python
import math
import jax
import jax.numpy as jnp
from jax import lax

D = 3584
HD = 128
KVH = 4
QH = 4
BS = 128
NV = 4
NS = 4
TOKENS = 32768
NB = 256


def draw_hidden_in(key, part):
    first_key = jax.random.fold_in(key, 11)
    values = jnp.clip(jax.random.normal(first_key, (TOKENS, D), jnp.float32), -4.0, 4.0)
    return values.astype(jnp.bfloat16)


def with_ends(drawn, own_key, least, top_value):
    extent = drawn.shape
    index_at = [jax.random.randint(jax.random.fold_in(own_key, axis), (), 0, extent[axis]) for axis in range(len(extent))]
    drawn = drawn.at[tuple(index_at)].set(least)
    longest = extent.index(max(extent))
    index_at[longest] = (index_at[longest] + 1) % extent[longest]
    return drawn.at[tuple(index_at)].set(top_value)


def block_levels(key, extent, cuts, smallest, largest):
    gain = 1.0
    for dim, parts in cuts:
        heights = jax.random.uniform(jax.random.fold_in(jax.random.fold_in(key, 6), dim), (parts,), jnp.float32, smallest / len(cuts), largest / len(cuts))
        gain = gain * jnp.repeat(jnp.exp(heights), extent[dim] // parts).reshape((-1,) + (1,) * (len(extent) - 1 - dim))
    return gain


def noise(key, extent, deviation, limit, pieces=(), held_as=jnp.bfloat16):
    factor_of = block_levels(key, extent, pieces, -0.22, 0.18) if pieces else 1.0
    entries = jax.random.normal(key, extent, jnp.float32) * deviation * factor_of
    return jnp.minimum(jnp.maximum(entries, -limit), limit).astype(held_as)


def setup_inputs(seed: int = 0) -> dict:
    streams_of = jax.random.split(jax.random.key(seed), 8)
    hidden_in = draw_hidden_in(jax.random.fold_in(streams_of[7], 71), 0)
    w_query = noise(streams_of[1], (D, KVH * QH * HD), D ** -0.5, 0.09375, ((1, 4),))
    w_key = noise(streams_of[2], (D, KVH * HD), D ** -0.5, 0.09375, ((1, 4),))
    w_value = noise(streams_of[3], (D, KVH * HD), D ** -0.5, 0.09375, ((1, 4),))
    w_output = noise(streams_of[4], (KVH * QH * HD, D), (KVH * QH * HD) ** -0.5, 0.125, ((0, 4),))
    vertical = with_ends(jax.random.randint(streams_of[5], (KVH, QH, NV), 0, NB), jax.random.fold_in(streams_of[5], 1), 0, NB - 1).astype(jnp.int32)
    slash_offsets = with_ends(jax.random.randint(streams_of[6], (KVH, QH, NS), 1, NB), jax.random.fold_in(streams_of[6], 1), 1, NB - 1).astype(jnp.int32)
    return dict(hidden_in=hidden_in, w_query=w_query, w_key=w_key, w_value=w_value, w_output=w_output, vertical=vertical, slash_offsets=slash_offsets)


THETA = 10000000.0

def rotate(values, positions):
    half = values.shape[-1] // 2
    freq = jnp.exp(-(jnp.arange(half, dtype=jnp.float32) * 2.0 / values.shape[-1]) * math.log(THETA))
    angle = positions.astype(jnp.float32)[:, None, None] * freq[None, None, :]
    cosine = jnp.cos(angle)
    sine = jnp.sin(angle)
    first = values[..., :half]
    second = values[..., half:]
    return jnp.concatenate([first * cosine - second * sine, second * cosine + first * sine], axis=-1)

def slot_table(qblocks, columns, offsets):
    lead = columns.shape[:-1]
    count = qblocks.shape[0]
    diag = jnp.broadcast_to(qblocks.astype(jnp.int32)[:, None], lead + (count, 1))
    back = qblocks.astype(jnp.int32)[:, None] - offsets[..., None, :]
    upright = jnp.broadcast_to(columns[..., None, :], lead + (count, columns.shape[-1]))
    slots = jnp.concatenate([diag, back, upright], axis=-1).astype(jnp.int32)
    width = slots.shape[-1]
    same = slots[..., :, None] == slots[..., None, :]
    lower = jnp.tril(jnp.ones((width, width), dtype=bool), -1)
    repeated = jnp.any(same & lower, axis=-1)
    valid = (slots >= 0) & (slots <= qblocks.astype(jnp.int32)[:, None]) & jnp.logical_not(repeated)
    return (jnp.maximum(slots, 0).astype(jnp.int32), valid)

def sparse_attend(query, key_blocks, value_blocks, qblocks, columns, offsets):
    heads, count, block, head_dim = query.shape
    slots, valid = slot_table(qblocks, columns, offsets)
    width = slots.shape[-1]
    picked_k = key_blocks[slots].reshape(heads, count, width * block, head_dim)
    picked_v = value_blocks[slots].reshape(heads, count, width * block, head_dim)
    scores = jnp.einsum('hbqd,hbkd->hbqk', query.astype(jnp.float32), picked_k.astype(jnp.float32)) / math.sqrt(head_dim)
    inner = jnp.arange(block, dtype=jnp.int32)
    qpos = qblocks.astype(jnp.int32)[:, None] * block + inner[None, :]
    kpos = (slots[..., None] * block + inner).reshape(heads, count, width * block)
    live = jnp.broadcast_to(valid[..., None], (heads, count, width, block)).reshape(heads, count, width * block)
    allowed = live[:, :, None, :] & (kpos[:, :, None, :] <= qpos[None, :, :, None])
    masked = jnp.where(allowed, scores, jnp.float32(-1e+30))
    top = lax.optimization_barrier(jnp.max(masked, axis=-1, keepdims=True))
    raw = jnp.where(allowed, jnp.exp(masked - top), jnp.float32(0.0))
    total = lax.optimization_barrier(jnp.sum(raw, axis=-1, keepdims=True))
    weights = raw.astype(jnp.bfloat16)
    summed = jnp.einsum('hbqk,hbkd->hbqd', weights.astype(jnp.float32), picked_v.astype(jnp.float32))
    return (summed / total).astype(jnp.bfloat16)

def reference(hidden_in, w_query, w_key, w_value, w_output, vertical, slash_offsets):
    tokens = hidden_in.shape[0]
    positions = jnp.arange(tokens, dtype=jnp.int32)
    proj_q = jnp.dot(hidden_in, w_query, preferred_element_type=jnp.float32).reshape(tokens, KVH * QH, HD)
    proj_k = jnp.dot(hidden_in, w_key, preferred_element_type=jnp.float32).reshape(tokens, KVH, HD)
    proj_v = jnp.dot(hidden_in, w_value, preferred_element_type=jnp.float32).reshape(tokens, KVH, HD)
    query = rotate(proj_q, positions).astype(jnp.bfloat16)
    keys = rotate(proj_k, positions).astype(jnp.bfloat16)
    values = proj_v.astype(jnp.bfloat16)
    key_blocks = keys.reshape(NB, BS, KVH, HD).transpose(2, 0, 1, 3)
    value_blocks = values.reshape(NB, BS, KVH, HD).transpose(2, 0, 1, 3)
    query_blocks = query.reshape(NB, BS, KVH, QH, HD).transpose(0, 2, 3, 1, 4)

    def one_block(inputs):
        block_index, qpart = inputs
        qblocks = jnp.reshape(block_index, (1,)).astype(jnp.int32)

        def per_group(qgroup, kgroup, vgroup, columns, offsets):
            return sparse_attend(qgroup[:, None], kgroup, vgroup, qblocks, columns, offsets)
        return jax.vmap(per_group)(qpart, key_blocks, value_blocks, vertical, slash_offsets)
    outputs = lax.map(one_block, (jnp.arange(NB, dtype=jnp.int32), query_blocks))
    context = outputs[:, :, :, 0].transpose(0, 3, 1, 2, 4).reshape(tokens, KVH * QH * HD)
    return jnp.dot(context, w_output, preferred_element_type=jnp.float32).astype(jnp.bfloat16)
```

```python
import functools
import math

import jax
import jax.numpy as jnp
from jax import lax
from jax.experimental import pallas as pl
from jax.experimental.pallas import tpu as pltpu
from jax.sharding import Mesh, PartitionSpec as P

BS = 128
THETA = 10000000.0
CHUNKS = 2
F32 = jnp.float32
BF16 = jnp.bfloat16
MIB = 1 << 20


def ring(n, step):
    return [(i, (i + step) % n) for i in range(n)]


def shift(x, axis, step):
    n = lax.axis_size(axis)
    return lax.ppermute(x, axis, ring(n, step))


def project_kernel(roped, at_ref, own, left, right, far_a, far_b, w, cos, sin, out):
    depth = own.shape[1]

    def rows(k):
        return w[pl.ds(pl.multiple_of(at_ref[k], 128), depth), :]

    total = jnp.dot(own[...], rows(0), preferred_element_type=F32)
    total += jnp.dot(left[...], rows(1), preferred_element_type=F32)
    total += jnp.dot(right[...], rows(2), preferred_element_type=F32)
    far = jnp.concatenate([far_a[...], far_b[...]], axis=0)
    total += jnp.dot(far, rows(3), preferred_element_type=F32)
    for head in range(total.shape[1] // BS):
        part = total[:, head * BS : (head + 1) * BS]
        if head < roped:
            turned = jnp.concatenate([part[:, BS // 2 :], part[:, : BS // 2]], axis=1)
            part = part * cos[...] + turned * sin[...]
        out[:, head * BS : (head + 1) * BS] = part.astype(BF16)


def project(at, pieces, w, cos, sin, roped):
    rows = pieces[0].shape[0]
    whole = pl.BlockSpec(memory_space=pltpu.VMEM)
    return pl.pallas_call(
        functools.partial(project_kernel, roped),
        out_shape=jax.ShapeDtypeStruct((rows, w.shape[1]), BF16),
        in_specs=[pl.BlockSpec(memory_space=pltpu.SMEM)] + [whole] * 8,
        out_specs=whole,
        compiler_params=pltpu.CompilerParams(vmem_limit_bytes=40 * MIB),
        cost_estimate=pl.CostEstimate(
            flops=2 * rows * w.shape[0] * w.shape[1],
            bytes_accessed=2 * (w.size + rows * w.shape[0] + rows * w.shape[1]),
            transcendentals=0,
        ),
    )(at, *pieces, w, cos, sin)


def attend_kernel(width, at_ref, ok_ref, q_ref, *refs):
    kv = refs[:width]
    out = refs[width]
    g, h = pl.program_id(0), pl.program_id(1)
    base = (g * pl.num_programs(1) + h) * width
    query = q_ref[...]
    scores = []
    for s in range(width):
        keys = kv[s][:, :BS]
        part = lax.dot_general(query, keys, (((1,), (1,)), ((), ())), preferred_element_type=F32)
        if s == 0:
            rows = lax.broadcasted_iota(jnp.int32, part.shape, 0)
            cols = lax.broadcasted_iota(jnp.int32, part.shape, 1)
            part = jnp.where(cols <= rows, part, -1e30)
        else:
            part = jnp.where(ok_ref[base + s] > 0, part, -1e30)
        scores.append(part)
    top = scores[0]
    for part in scores[1:]:
        top = jnp.maximum(top, part)
    top = jnp.max(top, axis=1, keepdims=True)
    scale = 1.0 / math.sqrt(BS)
    total = None
    summed = None
    for s in range(width):
        raw = jnp.exp((scores[s] - top) * scale)
        total = raw if total is None else total + raw
        term = jnp.dot(raw.astype(BF16), kv[s][:, BS:], preferred_element_type=F32)
        summed = term if summed is None else summed + term
    total = jnp.sum(total, axis=1, keepdims=True)
    out[...] = (summed / total).astype(BF16)


def attend(qsel, at, ok, query, kv_all):
    count, heads, width = at.shape

    def kv_spec(s):
        return pl.BlockSpec(
            (BS, 2 * BS),
            lambda g, h, at_r, ok_r, q_r: (at_r[(g * heads + h) * width + s], 0),
        )

    def kernel(at_ref, ok_ref, qsel_ref, *refs):
        attend_kernel(width, at_ref, ok_ref, *refs)

    return pl.pallas_call(
        kernel,
        grid_spec=pltpu.PrefetchScalarGridSpec(
            num_scalar_prefetch=3,
            grid=(count, heads),
            in_specs=[pl.BlockSpec((BS, BS), lambda g, h, at_r, ok_r, q_r: (q_r[g], h))]
            + [kv_spec(s) for s in range(width)],
            out_specs=pl.BlockSpec((BS, BS), lambda g, h, at_r, ok_r, q_r: (g, h)),
        ),
        out_shape=jax.ShapeDtypeStruct((count * BS, heads * BS), BF16),
        compiler_params=pltpu.CompilerParams(vmem_limit_bytes=32 * MIB),
        cost_estimate=pl.CostEstimate(
            flops=4 * count * heads * width * BS * BS * BS,
            bytes_accessed=4 * count * heads * width * BS * BS,
            transcendentals=count * heads * width * BS * BS,
        ),
    )(at.reshape(-1), ok.reshape(-1), qsel, query, *([kv_all] * width))


Z_ORDER = (0, 2, 4, 6, 7, 5, 3, 1)
Y_ORDER = (0, 2, 3, 1)


def slot_table(qblocks, columns, offsets):
    lead = columns.shape[:-1]
    count = qblocks.shape[0]
    diag = jnp.broadcast_to(qblocks[:, None], lead + (count, 1))
    back = qblocks[:, None] - offsets[..., None, :]
    upright = jnp.broadcast_to(columns[..., None, :], lead + (count, columns.shape[-1]))
    slots = jnp.concatenate([diag, back, upright], axis=-1)
    width = slots.shape[-1]
    same = slots[..., :, None] == slots[..., None, :]
    lower = jnp.tril(jnp.ones((width, width), dtype=bool), -1)
    repeated = jnp.any(same & lower, axis=-1)
    valid = (slots >= 0) & (slots <= qblocks[:, None]) & jnp.logical_not(repeated)
    return (jnp.maximum(slots, 0), valid)


def pick(table, index):
    out = jnp.full_like(index, table[0])
    for k in range(1, len(table)):
        out = jnp.where(index == k, table[k], out)
    return out


def place_of(block, z, y, c, per):
    owner, inner = block // 4, block % 4
    theirs_z, theirs_y, theirs_c = owner // 8, (owner // 2) % 4, owner % 2
    nb = per // 2
    chunk, rest = inner // per, inner % per
    colour, inner = rest // nb, rest % nb
    zo = pick(Z_ORDER, (theirs_z - z) % 8)
    yo = pick(Y_ORDER, (theirs_y - y) % 4)
    pos = jnp.where(colour == 0, zo * 4 + yo, yo * 8 + zo)
    swapped = (theirs_c != c).astype(jnp.int32)
    return (((swapped * (4 // per) + chunk) * 2 + colour) * 32 + pos) * nb + inner


def gather_kv(kv):
    half = kv.shape[0] // 2
    a, b = kv[:half], kv[half:]
    cat = jnp.concatenate([a, shift(a, "y", 1), shift(a, "y", -1), shift(a, "y", 2)], axis=0)
    plus, minus, first = cat, cat, [cat]
    for _ in range(3):
        plus, minus = shift(plus, "z", 1), shift(minus, "z", -1)
        first += [plus, minus]
    first += [shift(plus[: 2 * half], "z", 1), shift(minus[2 * half :], "z", -1)]

    plus, minus, line = b, b, [b]
    for _ in range(3):
        plus, minus = shift(plus, "z", 1), shift(minus, "z", -1)
        line += [plus, minus]
    line.append(shift(plus, "z", 1))
    cat = jnp.concatenate(line, axis=0)
    plus, minus = shift(cat, "y", 1), shift(cat, "y", -1)
    second = [cat, plus, minus]
    second += [shift(plus[: 4 * half], "y", 1), shift(minus[4 * half :], "y", -1)]
    return first, second


def body(hidden, w_query, w_key, w_value, w_output, vertical, slash_offsets):
    z, y, c, x = (lax.axis_index(a) for a in ("z", "y", "c", "x"))
    device = (z * 4 + y) * 2 + c
    tok_rows, depth = hidden.shape
    local = tok_rows // BS
    per = local // CHUNKS
    rows = tok_rows // CHUNKS

    half = BS // 2
    positions = device * tok_rows + jnp.arange(tok_rows, dtype=jnp.int32)
    freq = jnp.exp(-(jnp.arange(half, dtype=F32) * 2.0 / BS) * math.log(THETA))
    angle = positions.astype(F32)[:, None] * freq[None, :]
    cosine, sine = jnp.cos(angle), jnp.sin(angle)
    cos = jnp.concatenate([cosine, cosine], axis=1)
    sin = jnp.concatenate([-sine, sine], axis=1)
    w_kv = jnp.concatenate([w_key, w_value], axis=1)
    at = jnp.stack([x, (x + 3) % 4, (x + 1) % 4, (x + 2) % 4]).astype(jnp.int32) * depth

    queries, firsts, seconds = [], [], []
    for j in range(CHUNKS):
        own = hidden[j * rows : (j + 1) * rows]
        left, right = shift(own, "x", 1), shift(own, "x", -1)
        far_a = shift(left[: rows // 2], "x", 1)
        far_b = shift(right[rows // 2 :], "x", -1)
        pieces = (own, left, right, far_a, far_b)
        part = slice(j * rows, (j + 1) * rows)
        kv = project(at, pieces, w_kv, cos[part], sin[part], 1)
        queries.append(project(at, pieces, w_query, cos[part], sin[part], w_query.shape[1] // BS))
        first, second = gather_kv(kv)
        firsts.append(first)
        seconds.append(second)
    query = jnp.concatenate(queries, axis=0)

    arrays = [a for j in range(CHUNKS) for a in firsts[j] + seconds[j]]
    arrays += [shift(a, "c", 1) for a in arrays]
    kv_all = jnp.concatenate(arrays, axis=0)

    order = jnp.stack([(x + s) % 4 for s in (2, 1, 3, 0)]).astype(jnp.int32)
    slots, valid = slot_table(device * local + order, vertical[0], slash_offsets[0])
    places = place_of(slots, z, y, c, per).transpose(1, 0, 2)
    valid = valid.astype(jnp.int32).transpose(1, 0, 2)

    def share(first, last):
        part = slice(first, last)
        context = attend(order[part], places[part], valid[part], query, kv_all)
        return jnp.dot(context, w_output, preferred_element_type=F32)

    cut = w_output.shape[1] // 2
    far = share(0, 1).astype(BF16)
    from_left = shift(far[:, :cut], "x", 1).astype(F32)
    from_right = shift(far[:, cut:], "x", -1).astype(F32)
    near = share(1, 3)
    ahead, behind = near[:BS], near[BS:]
    ahead = jnp.concatenate([ahead[:, :cut] + from_left, ahead[:, cut:]], axis=1).astype(BF16)
    behind = jnp.concatenate([behind[:, :cut], behind[:, cut:] + from_right], axis=1).astype(BF16)
    ahead, behind = shift(ahead, "x", 1), shift(behind, "x", -1)
    mine = share(3, 4)
    return (mine + ahead.astype(F32) + behind.astype(F32)).astype(BF16)


def solution(mesh):
    fine = Mesh(mesh.devices.reshape(8, 4, 2, 4), ("z", "y", "c", "x"))
    ctx = ("z", "y", "c")
    placed = (
        P(ctx, "x"),
        P(None, "x"),
        P(None, "x"),
        P(None, "x"),
        P("x", None),
        P("x", None, None),
        P("x", None, None),
    )
    return jax.shard_map(
        body, mesh=fine, in_specs=placed, out_specs=P(ctx + ("x",), None), check_vma=False
    )
```

```python
import functools
import math

import jax
import jax.numpy as jnp
from jax import lax
from jax.experimental import pallas as pl
from jax.experimental.pallas import tpu as pltpu
from jax.sharding import Mesh, PartitionSpec as P

BS = 128
THETA = 10000000.0
F32 = jnp.float32
BF16 = jnp.bfloat16
MIB = 1 << 20
ANY = pl.BlockSpec(memory_space=pl.ANY)
VMEM = pl.BlockSpec(memory_space=pltpu.VMEM)
SMEM = pl.BlockSpec(memory_space=pltpu.SMEM)


def shift(x, axis, step):
    n = lax.axis_size(axis)
    return lax.ppermute(x, axis, [(i, (i + step) % n) for i in range(n)])


def tie(x, *after):
    def kernel(*refs):
        pass

    return pl.pallas_call(
        kernel,
        out_shape=jax.ShapeDtypeStruct(x.shape, x.dtype),
        in_specs=[ANY] * (1 + len(after)),
        out_specs=ANY,
        input_output_aliases={0: 0},
    )(x, *[a[:8, :BS] for a in after])


def project_kernel(roped, at_ref, own, left, right, far_a, far_b, w, cos, sin, out):
    depth = own.shape[1]

    def rows(k):
        return w[pl.ds(pl.multiple_of(at_ref[k], 128), depth), :]

    total = jnp.dot(own[...], rows(0), preferred_element_type=F32)
    total += jnp.dot(left[...], rows(1), preferred_element_type=F32)
    total += jnp.dot(right[...], rows(2), preferred_element_type=F32)
    far = jnp.concatenate([far_a[...], far_b[...]], axis=0)
    total += jnp.dot(far, rows(3), preferred_element_type=F32)
    for head in range(total.shape[1] // BS):
        part = total[:, head * BS : (head + 1) * BS]
        if head < roped:
            turned = jnp.concatenate([part[:, BS // 2 :], part[:, : BS // 2]], axis=1)
            part = part * cos[...] + turned * sin[...]
        out[:, head * BS : (head + 1) * BS] = part.astype(BF16)


def project(at, pieces, w, cos, sin, roped):
    rows = pieces[0].shape[0]
    return pl.pallas_call(
        functools.partial(project_kernel, roped),
        out_shape=jax.ShapeDtypeStruct((rows, w.shape[1]), BF16),
        in_specs=[SMEM] + [VMEM] * 8,
        out_specs=VMEM,
        compiler_params=pltpu.CompilerParams(vmem_limit_bytes=40 * MIB),
        cost_estimate=pl.CostEstimate(
            flops=2 * rows * w.shape[0] * w.shape[1],
            bytes_accessed=2 * (w.size + rows * w.shape[0] + rows * w.shape[1]),
            transcendentals=0,
        ),
    )(at, *pieces, w, cos, sin)


def attend_kernel(count, heads, width, lengths, at_ref, ok_ref, order_ref, q_ref, *refs):
    n = len(lengths)
    arrays, outs, held, sem = refs[:n], refs[n : n + count], refs[n + count], refs[n + count + 1]
    copies, row = [], 0
    for k in range(n):
        copies.append(
            pltpu.make_async_copy(arrays[k], held.at[pl.ds(row, lengths[k])], sem.at[k])
        )
        row += lengths[k]
    for copy in copies:
        copy.start()
    for copy in copies:
        copy.wait()
    scale = 1.0 / math.sqrt(BS)
    rows = lax.broadcasted_iota(jnp.int32, (BS, BS), 0)
    cols = lax.broadcasted_iota(jnp.int32, (BS, BS), 1)
    causal = cols <= rows
    for g in range(count):
        first = pl.multiple_of(order_ref[g] * BS, BS)
        for h in range(heads):
            base = (g * heads + h) * width
            query = q_ref[pl.ds(first, BS), h * BS : (h + 1) * BS]
            places = [pl.ds(pl.multiple_of(at_ref[base + s] * BS, BS), BS) for s in range(width)]
            scores = []
            for s in range(width):
                part = lax.dot_general(
                    query,
                    held[places[s], :BS],
                    (((1,), (1,)), ((), ())),
                    preferred_element_type=F32,
                )
                keep = causal if s == 0 else ok_ref[base + s] > 0
                scores.append(jnp.where(keep, part, -1e30))
            top = scores[0]
            for part in scores[1:]:
                top = jnp.maximum(top, part)
            top = jnp.max(top, axis=1, keepdims=True)
            total = None
            summed = None
            for s in range(width):
                raw = jnp.exp((scores[s] - top) * scale)
                total = raw if total is None else total + raw
                term = jnp.dot(raw.astype(BF16), held[places[s], BS:], preferred_element_type=F32)
                summed = term if summed is None else summed + term
            total = jnp.sum(total, axis=1, keepdims=True)
            outs[g][:, h * BS : (h + 1) * BS] = (summed / total).astype(BF16)


def attend(order, at, ok, query, arrays):
    count, heads, width = at.shape
    lengths = tuple(a.shape[0] for a in arrays)
    wide = arrays[0].shape[1]
    return pl.pallas_call(
        functools.partial(attend_kernel, count, heads, width, lengths),
        out_shape=[jax.ShapeDtypeStruct((BS, heads * BS), BF16)] * count,
        in_specs=[SMEM] * 3 + [VMEM] + [ANY] * len(arrays),
        out_specs=[VMEM] * count,
        scratch_shapes=[
            pltpu.VMEM((sum(lengths), wide), BF16),
            pltpu.SemaphoreType.DMA((len(arrays),)),
        ],
        compiler_params=pltpu.CompilerParams(vmem_limit_bytes=32 * MIB),
        cost_estimate=pl.CostEstimate(
            flops=4 * count * heads * width * BS * BS * BS,
            bytes_accessed=2 * sum(lengths) * wide,
            transcendentals=count * heads * width * BS * BS,
        ),
    )(at.reshape(-1), ok.reshape(-1), order, query, *arrays)


def output_kernel(mine, other, *refs):
    out_mine, out_other = refs[-2:]
    both = jnp.concatenate([mine[...], other[...]], axis=0)
    total, row = None, 0
    for w in refs[:-2]:
        term = jnp.dot(both[:, row : row + w.shape[0]], w[...], preferred_element_type=F32)
        total = term if total is None else total + term
        row += w.shape[0]
    total = total.astype(BF16)
    out_mine[...] = total[: mine.shape[0]]
    out_other[...] = total[mine.shape[0] :]


def output(mine, other, weights):
    rows, wide = mine.shape[0], weights[0].shape[1]
    size = sum(w.shape[0] for w in weights) * wide
    return pl.pallas_call(
        output_kernel,
        out_shape=[jax.ShapeDtypeStruct((rows, wide), BF16)] * 2,
        in_specs=[VMEM] * (2 + len(weights)),
        out_specs=[VMEM] * 2,
        compiler_params=pltpu.CompilerParams(vmem_limit_bytes=40 * MIB),
        cost_estimate=pl.CostEstimate(
            flops=4 * rows * size, bytes_accessed=2 * size, transcendentals=0
        ),
    )(mine, other, *weights)


Z_ORDER = (0, 2, 4, 6, 7, 5, 3, 1)
Y_ORDER = (0, 2, 3, 1)


def slot_table(qblocks, columns, offsets):
    lead = columns.shape[:-1]
    count = qblocks.shape[0]
    diag = jnp.broadcast_to(qblocks[:, None], lead + (count, 1))
    back = qblocks[:, None] - offsets[..., None, :]
    upright = jnp.broadcast_to(columns[..., None, :], lead + (count, columns.shape[-1]))
    slots = jnp.concatenate([diag, back, upright], axis=-1)
    width = slots.shape[-1]
    same = slots[..., :, None] == slots[..., None, :]
    lower = jnp.tril(jnp.ones((width, width), dtype=bool), -1)
    repeated = jnp.any(same & lower, axis=-1)
    valid = (slots >= 0) & (slots <= qblocks[:, None]) & jnp.logical_not(repeated)
    return (jnp.maximum(slots, 0), valid)


def pick(table, index):
    out = jnp.full_like(index, table[0])
    for k in range(1, len(table)):
        out = jnp.where(index == k, table[k], out)
    return out


def place_of(block, z, y, c):
    owner, inner = block // 4, block % 4
    theirs_z, theirs_y, theirs_c = owner // 8, (owner // 2) % 4, owner % 2
    zo = pick(Z_ORDER, (theirs_z - z) % 8)
    yo = pick(Y_ORDER, (theirs_y - y) % 4)
    chunk = inner // 2
    pos = jnp.where(chunk == 0, yo * 8 + zo, zo * 4 + yo)
    swapped = (theirs_c != c).astype(jnp.int32)
    return ((swapped * 2 + chunk) * 32 + pos) * 2 + inner % 2


def body(hidden, w_query, w_key, w_value, w_output, vertical, slash_offsets):
    z, y, c, x = (lax.axis_index(a) for a in ("z", "y", "c", "x"))
    device = (z * 4 + y) * 2 + c
    tok_rows, depth = hidden.shape
    local = tok_rows // BS
    rows = tok_rows // 2
    cut = w_output.shape[1] // 2

    half = BS // 2
    positions = device * tok_rows + jnp.arange(tok_rows, dtype=jnp.int32)
    freq = jnp.exp(-(jnp.arange(half, dtype=F32) * 2.0 / BS) * math.log(THETA))
    angle = positions.astype(F32)[:, None] * freq[None, :]
    cosine, sine = jnp.cos(angle), jnp.sin(angle)
    cos = jnp.concatenate([cosine, cosine], axis=1)
    sin = jnp.concatenate([-sine, sine], axis=1)
    w_kv = jnp.concatenate([w_key, w_value], axis=1)
    at = jnp.stack([x, (x + 3) % 4, (x + 1) % 4, (x + 2) % 4]).astype(jnp.int32) * depth
    w_own = lax.dynamic_slice_in_dim(w_output, c * cut, cut, axis=1)

    order = jnp.stack([(x + s) % 4 for s in range(local)]).astype(jnp.int32)
    slots, valid = slot_table(device * local + order, vertical[0], slash_offsets[0])
    places = place_of(slots, z, y, c).transpose(1, 0, 2)
    valid = valid.astype(jnp.int32).transpose(1, 0, 2)

    def swap(a):
        return shift(a, "c", 1)

    own0 = hidden[:rows]
    left0, right0 = shift(own0, "x", 1), shift(own0, "x", -1)
    far_a0, far_b0 = shift(left0[: rows // 2], "x", 1), shift(right0[rows // 2 :], "x", -1)
    pieces0 = (own0, left0, right0, far_a0, far_b0)
    own1 = tie(hidden[rows:], left0, right0)
    left1, right1 = shift(own1, "x", 1), shift(own1, "x", -1)

    kv0 = project(at, pieces0, w_kv, cos[:rows], sin[:rows], 1)
    plus, minus = shift(kv0, "z", 1), shift(kv0, "z", -1)
    line = [kv0, plus, minus]
    plus, minus = tie(plus, left1, right1), tie(minus, left1, right1)
    far_a1, far_b1 = shift(left1[: rows // 2], "x", 1), shift(right1[rows // 2 :], "x", -1)
    pieces1 = (own1, left1, right1, far_a1, far_b1)
    line = [kv0, plus, minus]
    plus, minus = shift(plus, "z", 1), shift(minus, "z", -1)
    plus, minus = tie(plus, far_a1, far_b1), tie(minus, far_a1, far_b1)
    line += [plus, minus]
    kv1 = project(at, pieces1, w_kv, cos[rows:], sin[rows:], 1)
    mid = w_own.shape[0] // 2
    w_own_a, w_own_b = tie(w_own[:mid], left1, right1), tie(w_own[mid:], left1, right1)
    w_left_a, w_right_b = shift(w_own_a, "x", 1), shift(w_own_b, "x", -1)

    plus, minus = shift(plus, "z", 1), shift(minus, "z", -1)
    line += [plus, minus]
    around = [kv1, shift(kv1, "y", 1), shift(kv1, "y", -1), shift(kv1, "y", 2)]
    line += [shift(plus[: rows // 2], "z", 1), shift(minus[rows // 2 :], "z", -1)]
    cat0 = jnp.concatenate(line, axis=0)
    cat1 = jnp.concatenate(around, axis=0)

    plus0, minus0 = shift(cat0, "y", 1), shift(cat0, "y", -1)
    plus, minus = shift(cat1, "z", 1), shift(cat1, "z", -1)
    plus, minus = tie(plus, w_left_a, w_right_b), tie(minus, w_left_a, w_right_b)
    second = [cat1, plus, minus]
    w_far_a, w_far_b = shift(w_left_a, "x", 1), shift(w_right_b, "x", -1)
    plus, minus = shift(plus, "z", 1), shift(minus, "z", -1)
    plus, minus = tie(plus, w_far_a, w_far_b), tie(minus, w_far_a, w_far_b)
    second += [plus, minus]
    w_left_b = shift(tie(w_own_b, w_far_a, w_far_b), "x", 1)
    w_right_a = shift(tie(w_own_a, w_far_a, w_far_b), "x", -1)
    top = cat0.shape[0] // 2
    first = [cat0, plus0, minus0]
    first += [shift(plus0[:top], "y", 1), shift(minus0[top:], "y", -1)]
    plus, minus = shift(plus, "z", 1), shift(minus, "z", -1)
    second += [plus, minus]
    top = cat1.shape[0] // 2
    second += [shift(plus[:top], "z", 1), shift(minus[top:], "z", -1)]

    wide = w_query.shape[1] // BS
    query = jnp.concatenate(
        [
            project(at, pieces0, w_query, cos[:rows], sin[:rows], wide),
            project(at, pieces1, w_query, cos[rows:], sin[rows:], wide),
        ],
        axis=0,
    )
    arrays = first + second
    arrays += [swap(a) for a in arrays]

    query = tie(query, w_left_b, w_right_a)
    own, ahead, across, behind = attend(order, places, valid, query, arrays)
    context = jnp.concatenate(
        [own, shift(ahead, "x", 1), shift(behind, "x", -1), shift(across, "x", 2)], axis=1
    )
    weights = (w_own_a, w_own_b, w_left_a, w_left_b, w_right_a, w_right_b, w_far_a, w_far_b)
    mine, theirs = output(context, swap(context), weights)
    theirs = swap(theirs)
    return jnp.where(
        c == 0,
        jnp.concatenate([mine, theirs], axis=1),
        jnp.concatenate([theirs, mine], axis=1),
    )


def solution(mesh):
    fine = Mesh(mesh.devices.reshape(8, 4, 2, 4), ("z", "y", "c", "x"))
    ctx = ("z", "y", "c")
    placed = (
        P(ctx, "x"),
        P(None, "x"),
        P(None, "x"),
        P(None, "x"),
        P("x", None),
        P("x", None, None),
        P("x", None, None),
    )
    return jax.shard_map(
        body, mesh=fine, in_specs=placed, out_specs=P(ctx + ("x",), None), check_vma=False
    )
```

```python
import functools
import math

import jax
import jax.numpy as jnp
from jax import lax
from jax.experimental import pallas as pl
from jax.experimental.pallas import tpu as pltpu
from jax.sharding import Mesh, PartitionSpec as P

BS = 128
THETA = 10000000.0
F32 = jnp.float32
BF16 = jnp.bfloat16
MIB = 1 << 20
ANY = pl.BlockSpec(memory_space=pl.ANY)
VMEM = pl.BlockSpec(memory_space=pltpu.VMEM)
SMEM = pl.BlockSpec(memory_space=pltpu.SMEM)


def shift(x, axis, step):
    n = lax.axis_size(axis)
    return lax.ppermute(x, axis, [(i, (i + step) % n) for i in range(n)])


def tie(x, *after):
    def kernel(*refs):
        pass

    return pl.pallas_call(
        kernel,
        out_shape=jax.ShapeDtypeStruct(x.shape, x.dtype),
        in_specs=[ANY] * (1 + len(after)),
        out_specs=ANY,
        input_output_aliases={0: 0},
        compiler_params=pltpu.CompilerParams(vmem_limit_bytes=MIB),
    )(x, *after)


def copy_rows(parts, outs, *after):
    arrays = [p[0] for p in parts]
    n = len(parts)

    def kernel(*refs):
        given, made, sem = refs[:n], refs[n + len(after) : -1], refs[-1]
        copies = []
        for k, (_, start, rows, to, row) in enumerate(parts):
            copies.append(
                pltpu.make_async_copy(
                    given[k].at[pl.ds(start, rows)], made[to].at[pl.ds(row, rows)], sem.at[k]
                )
            )
        for copy in copies:
            copy.start()
        for copy in copies:
            copy.wait()

    wide = arrays[0].shape[1]
    return pl.pallas_call(
        kernel,
        out_shape=[jax.ShapeDtypeStruct((r, wide), arrays[0].dtype) for r in outs],
        in_specs=[ANY] * (n + len(after)),
        out_specs=[ANY] * len(outs),
        scratch_shapes=[pltpu.SemaphoreType.DMA((n,))],
        compiler_params=pltpu.CompilerParams(vmem_limit_bytes=MIB),
        cost_estimate=pl.CostEstimate(
            flops=0, bytes_accessed=4 * wide * sum(p[2] for p in parts), transcendentals=0
        ),
    )(*arrays, *after)


def lay(*arrays):
    parts, row = [], 0
    for a in arrays:
        parts.append((a, 0, a.shape[0], 0, row))
        row += a.shape[0]
    return copy_rows(parts, [row])[0]


def halves(a, b, *after):
    half = a.shape[0] // 2
    return copy_rows([(a, 0, half, 0, 0), (b, half, half, 1, 0)], [half, half], *after)


def project_kernel(roped, at_ref, own, left, right, far, w, cos, sin, out):
    depth = own.shape[1]

    def rows(k):
        return w[pl.ds(pl.multiple_of(at_ref[k], 128), depth), :]

    total = jnp.dot(own[...], rows(0), preferred_element_type=F32)
    total += jnp.dot(left[...], rows(1), preferred_element_type=F32)
    total += jnp.dot(right[...], rows(2), preferred_element_type=F32)
    total += jnp.dot(far[...], rows(3), preferred_element_type=F32)
    for head in range(total.shape[1] // BS):
        part = total[:, head * BS : (head + 1) * BS]
        if head < roped:
            turned = jnp.concatenate([part[:, BS // 2 :], part[:, : BS // 2]], axis=1)
            part = part * cos[...] + turned * sin[...]
        out[:, head * BS : (head + 1) * BS] = part.astype(BF16)


def project(at, pieces, w, cos, sin, roped):
    rows = pieces[0].shape[0]
    return pl.pallas_call(
        functools.partial(project_kernel, roped),
        out_shape=jax.ShapeDtypeStruct((rows, w.shape[1]), BF16),
        in_specs=[SMEM] + [VMEM] * 7,
        out_specs=VMEM,
        compiler_params=pltpu.CompilerParams(vmem_limit_bytes=40 * MIB),
        cost_estimate=pl.CostEstimate(
            flops=2 * rows * w.shape[0] * w.shape[1],
            bytes_accessed=2 * (w.size + rows * w.shape[0] + rows * w.shape[1]),
            transcendentals=0,
        ),
    )(at, *pieces, w, cos, sin)


def attend_kernel(count, heads, width, lengths, at_ref, ok_ref, order_ref, q_ref, *refs):
    n = len(lengths)
    arrays, outs, held, sem = refs[:n], refs[n : n + count], refs[n + count], refs[n + count + 1]
    copies, row = [], 0
    for k in range(n):
        copies.append(
            pltpu.make_async_copy(arrays[k], held.at[pl.ds(row, lengths[k])], sem.at[k])
        )
        row += lengths[k]
    for copy in copies:
        copy.start()
    for copy in copies:
        copy.wait()
    scale = 1.0 / math.sqrt(BS)
    rows = lax.broadcasted_iota(jnp.int32, (BS, BS), 0)
    cols = lax.broadcasted_iota(jnp.int32, (BS, BS), 1)
    causal = cols <= rows
    for g in range(count):
        first = pl.multiple_of(order_ref[g] * BS, BS)
        for h in range(heads):
            base = (g * heads + h) * width
            query = q_ref[pl.ds(first, BS), h * BS : (h + 1) * BS]
            places = [pl.ds(pl.multiple_of(at_ref[base + s] * BS, BS), BS) for s in range(width)]
            scores = []
            for s in range(width):
                part = lax.dot_general(
                    query,
                    held[places[s], :BS],
                    (((1,), (1,)), ((), ())),
                    preferred_element_type=F32,
                )
                keep = causal if s == 0 else ok_ref[base + s] > 0
                scores.append(jnp.where(keep, part, -1e30))
            top = scores[0]
            for part in scores[1:]:
                top = jnp.maximum(top, part)
            top = jnp.max(top, axis=1, keepdims=True)
            total = None
            summed = None
            for s in range(width):
                raw = jnp.exp((scores[s] - top) * scale)
                total = raw if total is None else total + raw
                term = jnp.dot(raw.astype(BF16), held[places[s], BS:], preferred_element_type=F32)
                summed = term if summed is None else summed + term
            total = jnp.sum(total, axis=1, keepdims=True)
            outs[g][:, h * BS : (h + 1) * BS] = (summed / total).astype(BF16)


def attend(order, at, ok, query, arrays):
    count, heads, width = at.shape
    lengths = tuple(a.shape[0] for a in arrays)
    wide = arrays[0].shape[1]
    return pl.pallas_call(
        functools.partial(attend_kernel, count, heads, width, lengths),
        out_shape=[jax.ShapeDtypeStruct((BS, heads * BS), BF16)] * count,
        in_specs=[SMEM] * 3 + [VMEM] + [ANY] * len(arrays),
        out_specs=[VMEM] * count,
        scratch_shapes=[
            pltpu.VMEM((sum(lengths), wide), BF16),
            pltpu.SemaphoreType.DMA((len(arrays),)),
        ],
        compiler_params=pltpu.CompilerParams(vmem_limit_bytes=60 * MIB),
        cost_estimate=pl.CostEstimate(
            flops=4 * count * heads * width * BS * BS * BS,
            bytes_accessed=2 * sum(lengths) * wide,
            transcendentals=count * heads * width * BS * BS,
        ),
    )(at.reshape(-1), ok.reshape(-1), order, query, *arrays)


def output_kernel(group_ref, mine, other, w, out_mine, out_other):
    both = jnp.concatenate([mine[...], other[...]], axis=0)
    count = 4
    deep = w.shape[0] // count
    total = None
    for k in range(count):
        rows = pl.ds(pl.multiple_of(group_ref[k] * deep, deep), deep)
        term = jnp.dot(
            both[:, k * deep : (k + 1) * deep], w[rows, :], preferred_element_type=F32
        )
        total = term if total is None else total + term
    total = total.astype(BF16)
    out_mine[...] = total[: mine.shape[0]]
    out_other[...] = total[mine.shape[0] :]


def output(groups, mine, other, w):
    rows, wide = mine.shape[0], w.shape[1]
    return pl.pallas_call(
        output_kernel,
        out_shape=[jax.ShapeDtypeStruct((rows, wide), BF16)] * 2,
        in_specs=[SMEM] + [VMEM] * 3,
        out_specs=[VMEM] * 2,
        compiler_params=pltpu.CompilerParams(vmem_limit_bytes=40 * MIB),
        cost_estimate=pl.CostEstimate(
            flops=4 * rows * w.size, bytes_accessed=2 * w.size, transcendentals=0
        ),
    )(groups, mine, other, w)


Z_ORDER = (0, 2, 4, 6, 7, 5, 3, 1)
Y_ORDER = (0, 2, 3, 1)


def slot_table(qblocks, columns, offsets):
    lead = columns.shape[:-1]
    count = qblocks.shape[0]
    diag = jnp.broadcast_to(qblocks[:, None], lead + (count, 1))
    back = qblocks[:, None] - offsets[..., None, :]
    upright = jnp.broadcast_to(columns[..., None, :], lead + (count, columns.shape[-1]))
    slots = jnp.concatenate([diag, back, upright], axis=-1)
    width = slots.shape[-1]
    same = slots[..., :, None] == slots[..., None, :]
    lower = jnp.tril(jnp.ones((width, width), dtype=bool), -1)
    repeated = jnp.any(same & lower, axis=-1)
    valid = (slots >= 0) & (slots <= qblocks[:, None]) & jnp.logical_not(repeated)
    return (jnp.maximum(slots, 0), valid)


def pick(table, index):
    out = jnp.full_like(index, table[0])
    for k in range(1, len(table)):
        out = jnp.where(index == k, table[k], out)
    return out


def place_of(block, z, y, c):
    owner, inner = block // 4, block % 4
    theirs_z, theirs_y, theirs_c = owner // 8, (owner // 2) % 4, owner % 2
    zo = pick(Z_ORDER, (theirs_z - z) % 8)
    yo = pick(Y_ORDER, (theirs_y - y) % 4)
    chunk = inner // 2
    pos = jnp.where(chunk == 0, yo * 8 + zo, zo * 4 + yo)
    swapped = (theirs_c != c).astype(jnp.int32)
    return ((swapped * 2 + chunk) * 32 + pos) * 2 + inner % 2


def body(hidden, w_query, w_key, w_value, w_output, vertical, slash_offsets):
    z, y, c, x = (lax.axis_index(a) for a in ("z", "y", "c", "x"))
    device = (z * 4 + y) * 2 + c
    tok_rows, depth = hidden.shape
    local = tok_rows // BS
    rows = tok_rows // 2
    cut = w_output.shape[1] // 2

    half = BS // 2
    positions = device * tok_rows + jnp.arange(tok_rows, dtype=jnp.int32)
    freq = jnp.exp(-(jnp.arange(half, dtype=F32) * 2.0 / BS) * math.log(THETA))
    angle = positions.astype(F32)[:, None] * freq[None, :]
    cosine, sine = jnp.cos(angle), jnp.sin(angle)
    cos = jnp.concatenate([cosine, cosine], axis=1)
    sin = jnp.concatenate([-sine, sine], axis=1)
    w_kv = jnp.concatenate([w_key, w_value], axis=1)
    at = jnp.stack([x, (x + 3) % 4, (x + 1) % 4, (x + 2) % 4]).astype(jnp.int32) * depth
    w_own = lax.dynamic_slice_in_dim(w_output, c * cut, cut, axis=1)

    order = jnp.stack([(x + s) % 4 for s in range(local)]).astype(jnp.int32)
    slots, valid = slot_table(device * local + order, vertical[0], slash_offsets[0])
    places = place_of(slots, z, y, c).transpose(1, 0, 2)
    valid = valid.astype(jnp.int32).transpose(1, 0, 2)

    def swap(a):
        return shift(a, "c", 1)

    wide = w_query.shape[1] // BS

    own0 = hidden[:rows]
    pieces0 = (own0, shift(own0, "x", 1), shift(own0, "x", -1), shift(own0, "x", 2))
    own1 = tie(hidden[rows:], pieces0[3])
    pieces1 = (own1, shift(own1, "x", 1), shift(own1, "x", -1), shift(own1, "x", 2))

    kv0 = project(at, pieces0, w_kv, cos[:rows], sin[:rows], 1)
    plus, minus, line = kv0, kv0, [kv0]
    for _ in range(3):
        plus, minus = shift(plus, "z", 1), shift(minus, "z", -1)
        line += [plus, minus]
    line.append(shift(plus, "z", 1))
    query0 = project(at, pieces0, w_query, cos[:rows], tie(sin[:rows], kv0), wide)
    sin1 = tie(sin[rows:], query0, line[3], line[4])
    kv1 = project(at, pieces1, w_kv, cos[rows:], sin1, 1)
    around = [kv1] + [shift(kv1, "y", step) for step in (1, -1, 2)]
    query1 = project(at, pieces1, w_query, cos[rows:], tie(sin1, kv1), wide)
    query = lay(query0, query1)
    w_all = lax.all_gather(tie(w_own, kv1, line[-1]), "x", axis=0, tiled=True)

    cat1 = lay(*around)
    plus, minus = shift(cat1, "z", 1), shift(cat1, "z", -1)
    back = tie(minus, query)
    second = [cat1, plus, back]
    cat0 = lay(*line)
    above, below = shift(cat0, "y", 1), shift(cat0, "y", -1)
    plus, minus = shift(plus, "z", 1), shift(back, "z", -1)
    second += [plus, minus]
    plus, minus = shift(plus, "z", 1), shift(minus, "z", -1)
    second += [plus, minus]
    cat0 = tie(cat0, above, below)
    first = [cat0, above, below, shift(cat0, "y", 2)]
    top, bottom = halves(plus, minus)
    second += [shift(top, "z", 1), shift(bottom, "z", -1)]

    arrays = first + second
    arrays += [swap(a) for a in arrays]

    own, ahead, across, behind = attend(order, places, valid, query, arrays)
    context = jnp.concatenate(
        [own, shift(ahead, "x", 1), shift(behind, "x", -1), shift(across, "x", 2)], axis=1
    )
    mine, theirs = output(at // depth, context, swap(context), w_all)
    theirs = swap(theirs)
    return jnp.where(
        c == 0,
        jnp.concatenate([mine, theirs], axis=1),
        jnp.concatenate([theirs, mine], axis=1),
    )


def solution(mesh):
    fine = Mesh(mesh.devices.reshape(8, 4, 2, 4), ("z", "y", "c", "x"))
    ctx = ("z", "y", "c")
    placed = (
        P(ctx, "x"),
        P(None, "x"),
        P(None, "x"),
        P(None, "x"),
        P("x", None),
        P("x", None, None),
        P("x", None, None),
    )
    return jax.shard_map(
        body, mesh=fine, in_specs=placed, out_specs=P(ctx + ("x",), None), check_vma=False
    )
```

```python
import functools
import math

import jax
import jax.numpy as jnp
from jax import lax
from jax.experimental import pallas as pl
from jax.experimental.pallas import tpu as pltpu
from jax.sharding import Mesh, PartitionSpec as P

BS = 128
THETA = 10000000.0
F32 = jnp.float32
BF16 = jnp.bfloat16
MIB = 1 << 20
ANY = pl.BlockSpec(memory_space=pl.ANY)
VMEM = pl.BlockSpec(memory_space=pltpu.VMEM)
SMEM = pl.BlockSpec(memory_space=pltpu.SMEM)


def shift(x, axis, step):
    n = lax.axis_size(axis)
    return lax.ppermute(x, axis, [(i, (i + step) % n) for i in range(n)])


def tie(x, *after):
    def kernel(*refs):
        pass

    return pl.pallas_call(
        kernel,
        out_shape=jax.ShapeDtypeStruct(x.shape, x.dtype),
        in_specs=[ANY] * (1 + len(after)),
        out_specs=ANY,
        input_output_aliases={0: 0},
        compiler_params=pltpu.CompilerParams(vmem_limit_bytes=MIB),
    )(x, *after)


def copy_rows(parts, outs, *after):
    arrays = [p[0] for p in parts]
    n = len(parts)

    def kernel(*refs):
        given, made, sem = refs[:n], refs[n + len(after) : -1], refs[-1]
        copies = []
        for k, (_, start, rows, to, row) in enumerate(parts):
            copies.append(
                pltpu.make_async_copy(
                    given[k].at[pl.ds(start, rows)], made[to].at[pl.ds(row, rows)], sem.at[k]
                )
            )
        for copy in copies:
            copy.start()
        for copy in copies:
            copy.wait()

    wide = arrays[0].shape[1]
    return pl.pallas_call(
        kernel,
        out_shape=[jax.ShapeDtypeStruct((r, wide), arrays[0].dtype) for r in outs],
        in_specs=[ANY] * (n + len(after)),
        out_specs=[ANY] * len(outs),
        scratch_shapes=[pltpu.SemaphoreType.DMA((n,))],
        compiler_params=pltpu.CompilerParams(vmem_limit_bytes=MIB),
        cost_estimate=pl.CostEstimate(
            flops=0, bytes_accessed=4 * wide * sum(p[2] for p in parts), transcendentals=0
        ),
    )(*arrays, *after)


def lay(arrays, *after):
    parts, row = [], 0
    for a in arrays:
        parts.append((a, 0, a.shape[0], 0, row))
        row += a.shape[0]
    return copy_rows(parts, [row], *after)[0]


def halves(a, b, *after):
    half = a.shape[0] // 2
    return copy_rows([(a, 0, half, 0, 0), (b, half, half, 1, 0)], [half, half], *after)


def project_kernel(roped, at_ref, own, left, right, far, w, cos, sin, *refs):
    out = refs[-1]
    depth = own.shape[1]

    def rows(k):
        return w[pl.ds(pl.multiple_of(at_ref[k], 128), depth), :]

    total = jnp.dot(own[...], rows(0), preferred_element_type=F32)
    total += jnp.dot(left[...], rows(1), preferred_element_type=F32)
    total += jnp.dot(right[...], rows(2), preferred_element_type=F32)
    total += jnp.dot(far[...], rows(3), preferred_element_type=F32)
    for head in range(total.shape[1] // BS):
        part = total[:, head * BS : (head + 1) * BS]
        if head < roped:
            turned = jnp.concatenate([part[:, BS // 2 :], part[:, : BS // 2]], axis=1)
            part = part * cos[...] + turned * sin[...]
        out[:, head * BS : (head + 1) * BS] = part.astype(BF16)


def project(at, pieces, w, cos, sin, roped, *after):
    rows = pieces[0].shape[0]
    return pl.pallas_call(
        functools.partial(project_kernel, roped),
        out_shape=jax.ShapeDtypeStruct((rows, w.shape[1]), BF16),
        in_specs=[SMEM] + [VMEM] * 7 + [ANY] * len(after),
        out_specs=VMEM,
        compiler_params=pltpu.CompilerParams(vmem_limit_bytes=40 * MIB),
        cost_estimate=pl.CostEstimate(
            flops=2 * rows * w.shape[0] * w.shape[1],
            bytes_accessed=2 * (w.size + rows * w.shape[0] + rows * w.shape[1]),
            transcendentals=0,
        ),
    )(at, *pieces, w, cos, sin, *after)


def attend_kernel(count, heads, width, lengths, at_ref, ok_ref, order_ref, q_ref, *refs):
    n = len(lengths)
    arrays, outs, held, sem = refs[:n], refs[n : n + count], refs[n + count], refs[n + count + 1]
    copies, row = [], 0
    for k in range(n):
        copies.append(
            pltpu.make_async_copy(arrays[k], held.at[pl.ds(row, lengths[k])], sem.at[k])
        )
        row += lengths[k]
    for copy in copies:
        copy.start()
    for copy in copies:
        copy.wait()
    scale = 1.0 / math.sqrt(BS)
    rows = lax.broadcasted_iota(jnp.int32, (BS, BS), 0)
    cols = lax.broadcasted_iota(jnp.int32, (BS, BS), 1)
    causal = cols <= rows
    for g in range(count):
        first = pl.multiple_of(order_ref[g] * BS, BS)
        for h in range(heads):
            base = (g * heads + h) * width
            query = q_ref[pl.ds(first, BS), h * BS : (h + 1) * BS]
            places = [pl.ds(pl.multiple_of(at_ref[base + s] * BS, BS), BS) for s in range(width)]
            scores = []
            for s in range(width):
                part = lax.dot_general(
                    query,
                    held[places[s], :BS],
                    (((1,), (1,)), ((), ())),
                    preferred_element_type=F32,
                )
                keep = causal if s == 0 else ok_ref[base + s] > 0
                scores.append(jnp.where(keep, part, -1e30))
            top = scores[0]
            for part in scores[1:]:
                top = jnp.maximum(top, part)
            top = jnp.max(top, axis=1, keepdims=True)
            total = None
            summed = None
            for s in range(width):
                raw = jnp.exp((scores[s] - top) * scale)
                total = raw if total is None else total + raw
                term = jnp.dot(raw.astype(BF16), held[places[s], BS:], preferred_element_type=F32)
                summed = term if summed is None else summed + term
            total = jnp.sum(total, axis=1, keepdims=True)
            outs[g][:, h * BS : (h + 1) * BS] = (summed / total).astype(BF16)


def attend(order, at, ok, query, arrays):
    count, heads = order.shape[0], query.shape[1] // BS
    width = at.shape[0] // (count * heads)
    lengths = tuple(a.shape[0] for a in arrays)
    wide = arrays[0].shape[1]
    return pl.pallas_call(
        functools.partial(attend_kernel, count, heads, width, lengths),
        out_shape=[jax.ShapeDtypeStruct((BS, heads * BS), BF16)] * count,
        in_specs=[SMEM] * 3 + [VMEM] + [ANY] * len(arrays),
        out_specs=[VMEM] * count,
        scratch_shapes=[
            pltpu.VMEM((sum(lengths), wide), BF16),
            pltpu.SemaphoreType.DMA((len(arrays),)),
        ],
        compiler_params=pltpu.CompilerParams(vmem_limit_bytes=60 * MIB),
        cost_estimate=pl.CostEstimate(
            flops=4 * count * heads * width * BS * BS * BS,
            bytes_accessed=2 * sum(lengths) * wide,
            transcendentals=count * heads * width * BS * BS,
        ),
    )(at, ok, order, query, *arrays)


def output_kernel(group_ref, mine, other, w, out_mine, out_other, held, sem):
    count = sem.shape[0]
    deep = held.shape[0] // count
    copies = []
    for k in range(count):
        rows = pl.ds(pl.multiple_of(group_ref[k] * deep, deep), deep)
        copies.append(
            pltpu.make_async_copy(w.at[rows], held.at[pl.ds(k * deep, deep)], sem.at[k])
        )
    for copy in copies:
        copy.start()
    both = jnp.concatenate([mine[...], other[...]], axis=0)
    total = None
    for k in range(count):
        copies[k].wait()
        part = slice(k * deep, (k + 1) * deep)
        term = jnp.dot(both[:, part], held[part, :], preferred_element_type=F32)
        total = term if total is None else total + term
    total = total.astype(BF16)
    out_mine[...] = total[: mine.shape[0]]
    out_other[...] = total[mine.shape[0] :]


def output(groups, mine, other, w):
    rows, wide = mine.shape[0], w.shape[1]
    return pl.pallas_call(
        output_kernel,
        out_shape=[jax.ShapeDtypeStruct((rows, wide), BF16)] * 2,
        in_specs=[SMEM] + [VMEM] * 2 + [ANY],
        out_specs=[VMEM] * 2,
        scratch_shapes=[pltpu.VMEM(w.shape, BF16), pltpu.SemaphoreType.DMA(groups.shape)],
        compiler_params=pltpu.CompilerParams(vmem_limit_bytes=60 * MIB),
        cost_estimate=pl.CostEstimate(
            flops=4 * rows * w.size, bytes_accessed=2 * w.size, transcendentals=0
        ),
    )(groups, mine, other, w)


Z_ORDER = (0, 2, 4, 6, 7, 5, 3, 1)
Y_ORDER = (0, 2, 3, 1)


def slot_table(qblocks, columns, offsets):
    lead = columns.shape[:-1]
    count = qblocks.shape[0]
    diag = jnp.broadcast_to(qblocks[:, None], lead + (count, 1))
    back = qblocks[:, None] - offsets[..., None, :]
    upright = jnp.broadcast_to(columns[..., None, :], lead + (count, columns.shape[-1]))
    slots = jnp.concatenate([diag, back, upright], axis=-1)
    width = slots.shape[-1]
    same = slots[..., :, None] == slots[..., None, :]
    lower = jnp.tril(jnp.ones((width, width), dtype=bool), -1)
    repeated = jnp.any(same & lower, axis=-1)
    valid = (slots >= 0) & (slots <= qblocks[:, None]) & jnp.logical_not(repeated)
    return (jnp.maximum(slots, 0), valid)


def pick(table, index):
    out = jnp.full_like(index, table[0])
    for k in range(1, len(table)):
        out = jnp.where(index == k, table[k], out)
    return out


def place_of(block, z, y, c):
    owner, inner = block // 4, block % 4
    theirs_z, theirs_y, theirs_c = owner // 8, (owner // 2) % 4, owner % 2
    zo = pick(Z_ORDER, (theirs_z - z) % 8)
    yo = pick(Y_ORDER, (theirs_y - y) % 4)
    chunk = inner // 2
    pos = jnp.where(chunk == 0, yo * 8 + zo, zo * 4 + yo)
    swapped = (theirs_c != c).astype(jnp.int32)
    return ((swapped * 2 + chunk) * 32 + pos) * 2 + inner % 2


def body(hidden, w_query, w_key, w_value, w_output, vertical, slash_offsets):
    z, y, c, x = (lax.axis_index(a) for a in ("z", "y", "c", "x"))
    device = (z * 4 + y) * 2 + c
    tok_rows, depth = hidden.shape
    local = tok_rows // BS
    rows = tok_rows // 2
    cut = w_output.shape[1] // 2

    half = BS // 2
    positions = device * tok_rows + jnp.arange(tok_rows, dtype=jnp.int32)
    freq = jnp.exp(-(jnp.arange(half, dtype=F32) * 2.0 / BS) * math.log(THETA))
    angle = positions.astype(F32)[:, None] * freq[None, :]
    cosine, sine = jnp.cos(angle), jnp.sin(angle)
    cos = jnp.concatenate([cosine, cosine], axis=1)
    sin = jnp.concatenate([-sine, sine], axis=1)
    w_kv = jnp.concatenate([w_key, w_value], axis=1)
    at = jnp.stack([x, (x + 3) % 4, (x + 1) % 4, (x + 2) % 4]).astype(jnp.int32) * depth
    w_own = lax.dynamic_slice_in_dim(w_output, c * cut, cut, axis=1)

    order = jnp.stack([(x + s) % 4 for s in range(local)]).astype(jnp.int32)
    slots, valid = slot_table(device * local + order, vertical[0], slash_offsets[0])
    places = place_of(slots, z, y, c).transpose(1, 0, 2).reshape(-1)
    valid = valid.astype(jnp.int32).transpose(1, 0, 2).reshape(-1)

    def swap(a):
        return shift(a, "c", 1)

    wide = w_query.shape[1] // BS

    own0 = hidden[:rows]
    pieces0 = (own0, shift(own0, "x", 1), shift(own0, "x", -1), shift(own0, "x", 2))
    own1 = tie(hidden[rows:], pieces0[3], w_own, places, valid)
    pieces1 = (own1, shift(own1, "x", 1), shift(own1, "x", -1), shift(own1, "x", 2))

    kv0 = project(at, pieces0, w_kv, cos[:rows], sin[:rows], 1, own1)
    plus, minus, line = kv0, kv0, [kv0]
    for _ in range(3):
        plus, minus = shift(plus, "z", 1), shift(minus, "z", -1)
        line += [plus, minus]
    line.append(shift(plus, "z", 1))
    query0 = project(at, pieces0, w_query, cos[:rows], tie(sin[:rows], kv0), wide)
    sin1 = tie(sin[rows:], query0, line[3], line[4])
    kv1 = project(at, pieces1, w_kv, cos[rows:], sin1, 1)
    around = [kv1] + [shift(kv1, "y", step) for step in (1, -1, 2)]
    query1 = project(at, pieces1, w_query, cos[rows:], tie(sin1, kv1), wide)
    query = lay((query0, query1))
    w_all = lax.all_gather(tie(w_own, kv1, line[-1]), "x", axis=0, tiled=True)

    cat1 = lay(around, query)
    plus, minus = shift(cat1, "z", 1), shift(cat1, "z", -1)
    second = [cat1, plus, minus]
    cat0 = lay(line, cat1)
    above, below = shift(cat0, "y", 1), shift(cat0, "y", -1)
    plus, minus = shift(plus, "z", 1), shift(minus, "z", -1)
    second += [plus, minus]
    plus, minus = shift(plus, "z", 1), shift(minus, "z", -1)
    second += [plus, minus]
    cat0 = tie(cat0, above, below)
    first = [cat0, above, below, shift(cat0, "y", 2)]
    top, bottom = halves(plus, minus)
    second += [shift(top, "z", 1), shift(bottom, "z", -1)]

    arrays = first + second
    arrays += [swap(a) for a in arrays]

    own, ahead, across, behind = attend(order, places, valid, query, arrays)
    context = jnp.concatenate(
        [own, shift(ahead, "x", 1), shift(behind, "x", -1), shift(across, "x", 2)], axis=1
    )
    mine, theirs = output(at // depth, context, swap(context), w_all)
    theirs = swap(theirs)
    return jnp.where(
        c == 0,
        jnp.concatenate([mine, theirs], axis=1),
        jnp.concatenate([theirs, mine], axis=1),
    )


def solution(mesh):
    fine = Mesh(mesh.devices.reshape(8, 4, 2, 4), ("z", "y", "c", "x"))
    ctx = ("z", "y", "c")
    placed = (
        P(ctx, "x"),
        P(None, "x"),
        P(None, "x"),
        P(None, "x"),
        P("x", None),
        P("x", None, None),
        P("x", None, None),
    )
    return jax.shard_map(
        body, mesh=fine, in_specs=placed, out_specs=P(ctx + ("x",), None), check_vma=False
    )
```

```python
import functools
import math

import jax
import jax.numpy as jnp
from jax import lax
from jax.experimental import pallas as pl
from jax.experimental.pallas import tpu as pltpu
from jax.sharding import Mesh, PartitionSpec as P

BS = 128
THETA = 10000000.0
F32 = jnp.float32
BF16 = jnp.bfloat16
MIB = 1 << 20
ANY = pl.BlockSpec(memory_space=pl.ANY)
VMEM = pl.BlockSpec(memory_space=pltpu.VMEM)
SMEM = pl.BlockSpec(memory_space=pltpu.SMEM)
HBM = pl.BlockSpec(memory_space=pltpu.HBM)


def shift(x, axis, step):
    n = lax.axis_size(axis)
    return lax.ppermute(x, axis, [(i, (i + step) % n) for i in range(n)])


def tie(x, *after):
    def kernel(*refs):
        pass

    return pl.pallas_call(
        kernel,
        out_shape=jax.ShapeDtypeStruct(x.shape, x.dtype),
        in_specs=[ANY] * (1 + len(after)),
        out_specs=ANY,
        input_output_aliases={0: 0},
        compiler_params=pltpu.CompilerParams(vmem_limit_bytes=MIB),
    )(x, *after)


def copy_rows(parts, outs, *after):
    arrays = [p[0] for p in parts]
    n = len(parts)

    def kernel(*refs):
        given, made, sem = refs[:n], refs[n + len(after) : -1], refs[-1]
        copies = []
        for k, (_, start, rows, to, row) in enumerate(parts):
            copies.append(
                pltpu.make_async_copy(
                    given[k].at[pl.ds(start, rows)], made[to].at[pl.ds(row, rows)], sem.at[k]
                )
            )
        for copy in copies:
            copy.start()
        for copy in copies:
            copy.wait()

    wide = arrays[0].shape[1]
    return pl.pallas_call(
        kernel,
        out_shape=[jax.ShapeDtypeStruct((r, wide), arrays[0].dtype) for r in outs],
        in_specs=[ANY] * (n + len(after)),
        out_specs=[ANY] * len(outs),
        scratch_shapes=[pltpu.SemaphoreType.DMA((n,))],
        compiler_params=pltpu.CompilerParams(vmem_limit_bytes=MIB),
        cost_estimate=pl.CostEstimate(
            flops=0, bytes_accessed=4 * wide * sum(p[2] for p in parts), transcendentals=0
        ),
    )(*arrays, *after)


def lay(arrays, *after):
    parts, row = [], 0
    for a in arrays:
        parts.append((a, 0, a.shape[0], 0, row))
        row += a.shape[0]
    return copy_rows(parts, [row], *after)[0]


def project_kernel(roped, at_ref, own, left, right, far, w, cos, sin, *refs):
    out = refs[-1]
    depth = own.shape[1]

    def rows(k):
        return w[pl.ds(pl.multiple_of(at_ref[k], 128), depth), :]

    total = jnp.dot(own[...], rows(0), preferred_element_type=F32)
    total += jnp.dot(left[...], rows(1), preferred_element_type=F32)
    total += jnp.dot(right[...], rows(2), preferred_element_type=F32)
    total += jnp.dot(far[...], rows(3), preferred_element_type=F32)
    for head in range(total.shape[1] // BS):
        part = total[:, head * BS : (head + 1) * BS]
        if head < roped:
            turned = jnp.concatenate([part[:, BS // 2 :], part[:, : BS // 2]], axis=1)
            part = part * cos[...] + turned * sin[...]
        out[:, head * BS : (head + 1) * BS] = part.astype(BF16)


def project(at, pieces, w, cos, sin, roped, *after):
    rows = pieces[0].shape[0]
    return pl.pallas_call(
        functools.partial(project_kernel, roped),
        out_shape=jax.ShapeDtypeStruct((rows, w.shape[1]), BF16),
        in_specs=[SMEM] + [VMEM] * 7 + [ANY] * len(after),
        out_specs=VMEM,
        compiler_params=pltpu.CompilerParams(vmem_limit_bytes=40 * MIB),
        cost_estimate=pl.CostEstimate(
            flops=2 * rows * w.shape[0] * w.shape[1],
            bytes_accessed=2 * (w.size + rows * w.shape[0] + rows * w.shape[1]),
            transcendentals=0,
        ),
    )(at, *pieces, w, cos, sin, *after)


def attend_kernel(count, heads, width, parts, at_ref, ok_ref, order_ref, q_ref, *refs):
    n = len(parts)
    arrays, outs, held, sem = refs[:n], refs[n : n + count], refs[n + count], refs[n + count + 1]
    copies, row = [], 0
    for k, (start, rows) in enumerate(parts):
        copies.append(
            pltpu.make_async_copy(
                arrays[k].at[pl.ds(start, rows)], held.at[pl.ds(row, rows)], sem.at[k]
            )
        )
        row += rows
    for copy in copies:
        copy.start()
    for copy in copies:
        copy.wait()
    scale = math.log2(math.e) / math.sqrt(BS)
    rows = lax.broadcasted_iota(jnp.int32, (BS, BS), 0)
    cols = lax.broadcasted_iota(jnp.int32, (BS, BS), 1)
    causal = cols <= rows
    for g in range(count):
        first = pl.multiple_of(order_ref[g] * BS, BS)
        for h in range(heads):
            base = (g * heads + h) * width
            query = q_ref[pl.ds(first, BS), h * BS : (h + 1) * BS]
            places = [pl.ds(pl.multiple_of(at_ref[base + s] * BS, BS), BS) for s in range(width)]
            keys = jnp.concatenate([held[place, :BS] for place in places], axis=0)
            values = jnp.concatenate([held[place, BS:] for place in places], axis=0)
            product = lax.dot_general(
                query, keys, (((1,), (1,)), ((), ())), preferred_element_type=F32
            )
            scores = []
            for s in range(width):
                keep = causal if s == 0 else ok_ref[base + s] > 0
                scores.append(jnp.where(keep, product[:, s * BS : (s + 1) * BS], -1e30))
            top = scores[0]
            for part in scores[1:]:
                top = jnp.maximum(top, part)
            top = jnp.max(top, axis=1, keepdims=True)
            raw = [jnp.exp2((part - top) * scale) for part in scores]
            total = raw[0]
            for part in raw[1:]:
                total = total + part
            total = jnp.sum(total, axis=1, keepdims=True)
            weights = jnp.concatenate([part.astype(BF16) for part in raw], axis=1)
            summed = jnp.dot(weights, values, preferred_element_type=F32)
            outs[g][:, h * BS : (h + 1) * BS] = (summed / total).astype(BF16)


def attend(order, at, ok, query, pieces):
    count, heads = order.shape[0], query.shape[1] // BS
    width = at.shape[0] // (count * heads)
    arrays = [p[0] for p in pieces]
    parts = tuple(p[1:] for p in pieces)
    length = sum(p[2] for p in pieces)
    wide = arrays[0].shape[1]
    return pl.pallas_call(
        functools.partial(attend_kernel, count, heads, width, parts),
        out_shape=[jax.ShapeDtypeStruct((BS, heads * BS), BF16)] * count,
        in_specs=[SMEM] * 3 + [VMEM] + [HBM] * len(arrays),
        out_specs=[VMEM] * count,
        scratch_shapes=[
            pltpu.VMEM((length, wide), BF16),
            pltpu.SemaphoreType.DMA((len(arrays),)),
        ],
        compiler_params=pltpu.CompilerParams(vmem_limit_bytes=60 * MIB),
        cost_estimate=pl.CostEstimate(
            flops=4 * count * heads * width * BS * BS * BS,
            bytes_accessed=2 * length * wide,
            transcendentals=count * heads * width * BS * BS,
        ),
    )(at, ok, order, query, *arrays)


def output_kernel(group_ref, mine, other, w, out_mine, out_other):
    both = jnp.concatenate([mine[...], other[...]], axis=0)
    count = group_ref.shape[0]
    deep = w.shape[0] // count
    total = None
    for k in range(count):
        rows = pl.ds(pl.multiple_of(group_ref[k] * deep, deep), deep)
        term = jnp.dot(
            both[:, k * deep : (k + 1) * deep], w[rows, :], preferred_element_type=F32
        )
        total = term if total is None else total + term
    total = total.astype(BF16)
    out_mine[...] = total[: mine.shape[0]]
    out_other[...] = total[mine.shape[0] :]


def output(groups, mine, other, w):
    rows, wide = mine.shape[0], w.shape[1]
    return pl.pallas_call(
        output_kernel,
        out_shape=[jax.ShapeDtypeStruct((rows, wide), BF16)] * 2,
        in_specs=[SMEM] + [VMEM] * 3,
        out_specs=[VMEM] * 2,
        compiler_params=pltpu.CompilerParams(vmem_limit_bytes=20 * MIB),
        cost_estimate=pl.CostEstimate(
            flops=4 * rows * w.size, bytes_accessed=2 * w.size, transcendentals=0
        ),
    )(groups, mine, other, w)


def join_kernel(core_ref, mine, theirs, out, sem):
    wide = mine.shape[1]
    first = pl.ds(pl.multiple_of(core_ref[0] * wide, BS), wide)
    second = pl.ds(pl.multiple_of((1 - core_ref[0]) * wide, BS), wide)
    copies = [
        pltpu.make_async_copy(mine, out.at[:, first], sem.at[0]),
        pltpu.make_async_copy(theirs, out.at[:, second], sem.at[1]),
    ]
    for copy in copies:
        copy.start()
    for copy in copies:
        copy.wait()


def join(core, mine, theirs):
    return pl.pallas_call(
        join_kernel,
        out_shape=jax.ShapeDtypeStruct((mine.shape[0], 2 * mine.shape[1]), BF16),
        in_specs=[SMEM, ANY, ANY],
        out_specs=ANY,
        scratch_shapes=[pltpu.SemaphoreType.DMA((2,))],
        compiler_params=pltpu.CompilerParams(vmem_limit_bytes=MIB),
    )(core, mine, theirs)


Z_ORDER = (0, 2, 4, 6, 7, 5, 3, 1)
Y_ORDER = (0, 2, 3, 1)


def slot_table(qblocks, columns, offsets):
    lead = columns.shape[:-1]
    count = qblocks.shape[0]
    diag = jnp.broadcast_to(qblocks[:, None], lead + (count, 1))
    back = qblocks[:, None] - offsets[..., None, :]
    upright = jnp.broadcast_to(columns[..., None, :], lead + (count, columns.shape[-1]))
    slots = jnp.concatenate([diag, back, upright], axis=-1)
    width = slots.shape[-1]
    same = slots[..., :, None] == slots[..., None, :]
    lower = jnp.tril(jnp.ones((width, width), dtype=bool), -1)
    repeated = jnp.any(same & lower, axis=-1)
    valid = (slots >= 0) & (slots <= qblocks[:, None]) & jnp.logical_not(repeated)
    return (jnp.maximum(slots, 0), valid)


def pick(table, index):
    out = jnp.full_like(index, table[0])
    for k in range(1, len(table)):
        out = jnp.where(index == k, table[k], out)
    return out


def place_of(block, z, y, c):
    owner, inner = block // 4, block % 4
    theirs_z, theirs_y, theirs_c = owner // 8, (owner // 2) % 4, owner % 2
    zo = pick(Z_ORDER, (theirs_z - z) % 8)
    yo = pick(Y_ORDER, (theirs_y - y) % 4)
    chunk = inner // 2
    pos = jnp.where(chunk == 0, yo * 8 + zo, zo * 4 + yo)
    swapped = (theirs_c != c).astype(jnp.int32)
    return ((swapped * 2 + chunk) * 32 + pos) * 2 + inner % 2


def body(hidden, w_query, w_key, w_value, w_output, vertical, slash_offsets):
    z, y, c, x = (lax.axis_index(a) for a in ("z", "y", "c", "x"))
    device = (z * 4 + y) * 2 + c
    tok_rows, depth = hidden.shape
    local = tok_rows // BS
    rows = tok_rows // 2
    cut = w_output.shape[1] // 2

    half = BS // 2
    positions = device * tok_rows + jnp.arange(tok_rows, dtype=jnp.int32)
    freq = jnp.exp(-(jnp.arange(half, dtype=F32) * 2.0 / BS) * math.log(THETA))
    angle = positions.astype(F32)[:, None] * freq[None, :]
    cosine, sine = jnp.cos(angle), jnp.sin(angle)
    cos = jnp.concatenate([cosine, cosine], axis=1)
    sin = jnp.concatenate([-sine, sine], axis=1)
    w_kv = jnp.concatenate([w_key, w_value], axis=1)
    at = jnp.stack([x, (x + 3) % 4, (x + 1) % 4, (x + 2) % 4]).astype(jnp.int32) * depth
    w_own = lax.dynamic_slice_in_dim(w_output, c * cut, cut, axis=1)

    order = jnp.stack([(x + s) % 4 for s in range(local)]).astype(jnp.int32)
    slots, valid = slot_table(device * local + order, vertical[0], slash_offsets[0])
    places = place_of(slots, z, y, c).transpose(1, 0, 2).reshape(-1)
    valid = valid.astype(jnp.int32).transpose(1, 0, 2).reshape(-1)

    def swap(a):
        return shift(a, "c", 1)

    wide = w_query.shape[1] // BS

    own0 = hidden[:rows]
    pieces0 = (own0, shift(own0, "x", 1), shift(own0, "x", -1), shift(own0, "x", 2))
    own1 = hidden[rows:]
    pieces1 = (own1, shift(own1, "x", 1), shift(own1, "x", -1), shift(own1, "x", 2))

    kv0 = project(at, pieces0, w_kv, cos[:rows], sin[:rows], 1, w_own, places, valid)
    plus, minus, line = kv0, kv0, [kv0]
    query0 = project(at, pieces0, w_query, cos[:rows], tie(sin[:rows], kv0), wide)
    for k in range(3):
        plus, minus = shift(plus, "z", 1), shift(minus, "z", -1)
        if k == 1:
            minus = tie(minus, query0)
        line += [plus, minus]
    line.append(shift(plus, "z", 1))
    sin1 = tie(sin[rows:], line[3], line[4])
    kv1 = project(at, pieces1, w_kv, cos[rows:], sin1, 1)
    around = [kv1] + [shift(kv1, "y", step) for step in (1, -1, 2)]
    query1 = project(at, pieces1, w_query, cos[rows:], tie(sin1, kv1), wide)
    query = lay((query0, query1))
    w_all = lax.all_gather(tie(w_own, kv1, line[-1]), "x", axis=0, tiled=True)

    cat1 = lay(around, query)
    plus, minus, second = cat1, cat1, [cat1]
    cat0 = lay(line, cat1)
    above, below = shift(cat0, "y", 1), shift(cat0, "y", -1)
    for _ in range(3):
        plus, minus = shift(plus, "z", 1), shift(minus, "z", -1)
        second += [plus, minus]
    second.append(shift(plus, "z", 1))
    cat0 = tie(cat0, above, below)
    first = [cat0, above, below, shift(cat0, "y", 2)]

    arrays = first + second
    arrays += [swap(a) for a in arrays]
    pieces = [(a, 0, a.shape[0]) for a in arrays]
    query = tie(query, w_all)
    own, ahead, across, behind = attend(order, places, valid, query, pieces)
    context = jnp.concatenate(
        [own, shift(ahead, "x", 1), shift(behind, "x", -1), shift(across, "x", 2)], axis=1
    )
    mine, theirs = output(at // depth, context, swap(context), w_all)
    return join(jnp.reshape(c, (1,)).astype(jnp.int32), mine, swap(theirs))


def solution(mesh):
    fine = Mesh(mesh.devices.reshape(8, 4, 2, 4), ("z", "y", "c", "x"))
    ctx = ("z", "y", "c")
    placed = (
        P(ctx, "x"),
        P(None, "x"),
        P(None, "x"),
        P(None, "x"),
        P("x", None),
        P("x", None, None),
        P("x", None, None),
    )
    return jax.shard_map(
        body, mesh=fine, in_specs=placed, out_specs=P(ctx + ("x",), None), check_vma=False
    )
```

```python
import functools
import math

import jax
import jax.numpy as jnp
from jax import lax
from jax.experimental import pallas as pl
from jax.experimental.pallas import tpu as pltpu
from jax.sharding import Mesh, PartitionSpec as P

BS = 128
THETA = 10000000.0
F32 = jnp.float32
BF16 = jnp.bfloat16
MIB = 1 << 20
ANY = pl.BlockSpec(memory_space=pl.ANY)
VMEM = pl.BlockSpec(memory_space=pltpu.VMEM)
SMEM = pl.BlockSpec(memory_space=pltpu.SMEM)
HBM = pl.BlockSpec(memory_space=pltpu.HBM)


def shift(x, axis, step):
    n = lax.axis_size(axis)
    return lax.ppermute(x, axis, [(i, (i + step) % n) for i in range(n)])


def tie(x, *after):
    def kernel(*refs):
        pass

    return pl.pallas_call(
        kernel,
        out_shape=jax.ShapeDtypeStruct(x.shape, x.dtype),
        in_specs=[ANY] * (1 + len(after)),
        out_specs=ANY,
        input_output_aliases={0: 0},
        compiler_params=pltpu.CompilerParams(vmem_limit_bytes=MIB),
    )(x, *after)


def copy_rows(parts, outs, *after):
    arrays = [p[0] for p in parts]
    n = len(parts)

    def kernel(*refs):
        given, made, sem = refs[:n], refs[n + len(after) : -1], refs[-1]
        copies = []
        for k, (_, start, rows, to, row) in enumerate(parts):
            copies.append(
                pltpu.make_async_copy(
                    given[k].at[pl.ds(start, rows)], made[to].at[pl.ds(row, rows)], sem.at[k]
                )
            )
        for copy in copies:
            copy.start()
        for copy in copies:
            copy.wait()

    wide = arrays[0].shape[1]
    return pl.pallas_call(
        kernel,
        out_shape=[jax.ShapeDtypeStruct((r, wide), arrays[0].dtype) for r in outs],
        in_specs=[ANY] * (n + len(after)),
        out_specs=[ANY] * len(outs),
        scratch_shapes=[pltpu.SemaphoreType.DMA((n,))],
        compiler_params=pltpu.CompilerParams(vmem_limit_bytes=MIB),
        cost_estimate=pl.CostEstimate(
            flops=0, bytes_accessed=4 * wide * sum(p[2] for p in parts), transcendentals=0
        ),
    )(*arrays, *after)


def lay(arrays, *after):
    parts, row = [], 0
    for a in arrays:
        parts.append((a, 0, a.shape[0], 0, row))
        row += a.shape[0]
    return copy_rows(parts, [row], *after)[0]


def halves(a, b, *after):
    half = a.shape[0] // 2
    return copy_rows([(a, 0, half, 0, 0), (b, half, half, 1, 0)], [half, half], *after)


def project_kernel(
    roped, count, at_ref, own, left, right, far_a, far_b, w, cos, sin, *refs
):
    outs = refs[-count:]
    depth = own.shape[1]
    part_rows = own.shape[0] // count

    def rows(k):
        return w[pl.ds(pl.multiple_of(at_ref[k], 128), depth), :]

    total = jnp.dot(own[...], rows(0), preferred_element_type=F32)
    total += jnp.dot(left[...], rows(1), preferred_element_type=F32)
    total += jnp.dot(right[...], rows(2), preferred_element_type=F32)
    far = jnp.concatenate([far_a[...], far_b[...]], axis=0)
    total += jnp.dot(far, rows(3), preferred_element_type=F32)
    for head in range(total.shape[1] // BS):
        columns = slice(head * BS, (head + 1) * BS)
        part = total[:, columns]
        if head < roped:
            turned = jnp.concatenate([part[:, BS // 2 :], part[:, : BS // 2]], axis=1)
            part = part * cos[...] + turned * sin[...]
        part = part.astype(BF16)
        for k in range(count):
            outs[k][:, columns] = part[k * part_rows : (k + 1) * part_rows]


def project(at, pieces, w, cos, sin, roped, count, *after):
    rows = pieces[0].shape[0]
    return pl.pallas_call(
        functools.partial(project_kernel, roped, count),
        out_shape=[jax.ShapeDtypeStruct((rows // count, w.shape[1]), BF16)] * count,
        in_specs=[SMEM] + [VMEM] * 8 + [ANY] * len(after),
        out_specs=[VMEM] * count,
        compiler_params=pltpu.CompilerParams(vmem_limit_bytes=30 * MIB),
        cost_estimate=pl.CostEstimate(
            flops=2 * rows * w.shape[0] * w.shape[1],
            bytes_accessed=2 * (w.size + rows * w.shape[0] + rows * w.shape[1]),
            transcendentals=0,
        ),
    )(at, *pieces, w, cos, sin, *after)


def attend_kernel(count, heads, width, parts, at_ref, ok_ref, order_ref, q_ref, *refs):
    n = len(parts)
    arrays, outs, held, sem = refs[:n], refs[n : n + count], refs[n + count], refs[n + count + 1]
    copies, row = [], 0
    for k, (start, rows) in enumerate(parts):
        copies.append(
            pltpu.make_async_copy(
                arrays[k].at[pl.ds(start, rows)], held.at[pl.ds(row, rows)], sem.at[k]
            )
        )
        row += rows
    for copy in copies:
        copy.start()
    for copy in copies:
        copy.wait()
    scale = math.log2(math.e) / math.sqrt(BS)
    rows = lax.broadcasted_iota(jnp.int32, (BS, BS), 0)
    cols = lax.broadcasted_iota(jnp.int32, (BS, BS), 1)
    causal = cols <= rows
    for g in range(count):
        first = pl.multiple_of(order_ref[g] * BS, BS)
        for h in range(heads):
            base = (g * heads + h) * width
            query = q_ref[pl.ds(first, BS), h * BS : (h + 1) * BS]
            places = [pl.ds(pl.multiple_of(at_ref[base + s] * BS, BS), BS) for s in range(width)]
            keys = jnp.concatenate([held[place, :BS] for place in places], axis=0)
            values = jnp.concatenate([held[place, BS:] for place in places], axis=0)
            product = lax.dot_general(
                query, keys, (((1,), (1,)), ((), ())), preferred_element_type=F32
            )
            scores = []
            for s in range(width):
                keep = causal if s == 0 else ok_ref[base + s] > 0
                scores.append(jnp.where(keep, product[:, s * BS : (s + 1) * BS], -1e30))
            top = scores[0]
            for part in scores[1:]:
                top = jnp.maximum(top, part)
            top = jnp.max(top, axis=1, keepdims=True)
            raw = [jnp.exp2((part - top) * scale) for part in scores]
            total = raw[0]
            for part in raw[1:]:
                total = total + part
            total = jnp.sum(total, axis=1, keepdims=True)
            weights = jnp.concatenate([part.astype(BF16) for part in raw], axis=1)
            summed = jnp.dot(weights, values, preferred_element_type=F32)
            outs[g][:, h * BS : (h + 1) * BS] = (summed / total).astype(BF16)


def attend(order, at, ok, query, pieces):
    count, heads = order.shape[0], query.shape[1] // BS
    width = at.shape[0] // (count * heads)
    arrays = [p[0] for p in pieces]
    parts = tuple(p[1:] for p in pieces)
    length = sum(p[2] for p in pieces)
    wide = arrays[0].shape[1]
    return pl.pallas_call(
        functools.partial(attend_kernel, count, heads, width, parts),
        out_shape=[jax.ShapeDtypeStruct((BS, heads * BS), BF16)] * count,
        in_specs=[SMEM] * 3 + [VMEM] + [HBM] * len(arrays),
        out_specs=[VMEM] * count,
        scratch_shapes=[
            pltpu.VMEM((length, wide), BF16),
            pltpu.SemaphoreType.DMA((len(arrays),)),
        ],
        compiler_params=pltpu.CompilerParams(vmem_limit_bytes=60 * MIB),
        cost_estimate=pl.CostEstimate(
            flops=4 * count * heads * width * BS * BS * BS,
            bytes_accessed=2 * length * wide,
            transcendentals=count * heads * width * BS * BS,
        ),
    )(at, ok, order, query, *arrays)


def output_kernel(group_ref, mine, other, w, out_mine, out_other):
    both = jnp.concatenate([mine[...], other[...]], axis=0)
    count = group_ref.shape[0]
    deep = w.shape[0] // count
    total = None
    for k in range(count):
        rows = pl.ds(pl.multiple_of(group_ref[k] * deep, deep), deep)
        term = jnp.dot(
            both[:, k * deep : (k + 1) * deep], w[rows, :], preferred_element_type=F32
        )
        total = term if total is None else total + term
    total = total.astype(BF16)
    out_mine[...] = total[: mine.shape[0]]
    out_other[...] = total[mine.shape[0] :]


def output(groups, mine, other, w):
    rows, wide = mine.shape[0], w.shape[1]
    return pl.pallas_call(
        output_kernel,
        out_shape=[jax.ShapeDtypeStruct((rows, wide), BF16)] * 2,
        in_specs=[SMEM] + [VMEM] * 3,
        out_specs=[VMEM] * 2,
        compiler_params=pltpu.CompilerParams(vmem_limit_bytes=20 * MIB),
        cost_estimate=pl.CostEstimate(
            flops=4 * rows * w.size, bytes_accessed=2 * w.size, transcendentals=0
        ),
    )(groups, mine, other, w)


def join_kernel(core_ref, mine, theirs, out, sem):
    wide = mine.shape[1]
    first = pl.ds(pl.multiple_of(core_ref[0] * wide, BS), wide)
    second = pl.ds(pl.multiple_of((1 - core_ref[0]) * wide, BS), wide)
    copies = [
        pltpu.make_async_copy(mine, out.at[:, first], sem.at[0]),
        pltpu.make_async_copy(theirs, out.at[:, second], sem.at[1]),
    ]
    for copy in copies:
        copy.start()
    for copy in copies:
        copy.wait()


def join(core, mine, theirs):
    return pl.pallas_call(
        join_kernel,
        out_shape=jax.ShapeDtypeStruct((mine.shape[0], 2 * mine.shape[1]), BF16),
        in_specs=[SMEM, ANY, ANY],
        out_specs=ANY,
        scratch_shapes=[pltpu.SemaphoreType.DMA((2,))],
        compiler_params=pltpu.CompilerParams(vmem_limit_bytes=MIB),
    )(core, mine, theirs)


Z_ORDER = (0, 2, 4, 6, 7, 5, 3, 1)
Y_ORDER = (0, 2, 3, 1)


def slot_table(qblocks, columns, offsets):
    lead = columns.shape[:-1]
    count = qblocks.shape[0]
    diag = jnp.broadcast_to(qblocks[:, None], lead + (count, 1))
    back = qblocks[:, None] - offsets[..., None, :]
    upright = jnp.broadcast_to(columns[..., None, :], lead + (count, columns.shape[-1]))
    slots = jnp.concatenate([diag, back, upright], axis=-1)
    width = slots.shape[-1]
    same = slots[..., :, None] == slots[..., None, :]
    lower = jnp.tril(jnp.ones((width, width), dtype=bool), -1)
    repeated = jnp.any(same & lower, axis=-1)
    valid = (slots >= 0) & (slots <= qblocks[:, None]) & jnp.logical_not(repeated)
    return (jnp.maximum(slots, 0), valid)


def pick(table, index):
    out = jnp.full_like(index, table[0])
    for k in range(1, len(table)):
        out = jnp.where(index == k, table[k], out)
    return out


def place_of(block, z, y, c):
    owner, inner = block // 4, block % 4
    theirs_z, theirs_y, theirs_c = owner // 8, (owner // 2) % 4, owner % 2
    zo = pick(Z_ORDER, (theirs_z - z) % 8)
    yo = pick(Y_ORDER, (theirs_y - y) % 4)
    chunk = inner // 2
    pos = jnp.where(chunk == 0, yo * 8 + zo, zo * 4 + yo)
    swapped = (theirs_c != c).astype(jnp.int32)
    return ((swapped * 2 + chunk) * 32 + pos) * 2 + inner % 2


def body(hidden, w_query, w_key, w_value, w_output, vertical, slash_offsets):
    z, y, c, x = (lax.axis_index(a) for a in ("z", "y", "c", "x"))
    device = (z * 4 + y) * 2 + c
    tok_rows, depth = hidden.shape
    local = tok_rows // BS
    cut = w_output.shape[1] // 2

    half = BS // 2
    positions = device * tok_rows + jnp.arange(tok_rows, dtype=jnp.int32)
    freq = jnp.exp(-(jnp.arange(half, dtype=F32) * 2.0 / BS) * math.log(THETA))
    angle = positions.astype(F32)[:, None] * freq[None, :]
    cosine, sine = jnp.cos(angle), jnp.sin(angle)
    cos = jnp.concatenate([cosine, cosine], axis=1)
    sin = jnp.concatenate([-sine, sine], axis=1)
    w_kv = jnp.concatenate([w_key, w_value], axis=1)
    at = jnp.stack([x, (x + 3) % 4, (x + 1) % 4, (x + 2) % 4]).astype(jnp.int32) * depth
    w_own = lax.dynamic_slice_in_dim(w_output, c * cut, cut, axis=1)

    order = jnp.stack([(x + s) % 4 for s in range(local)]).astype(jnp.int32)
    slots, valid = slot_table(device * local + order, vertical[0], slash_offsets[0])
    places = place_of(slots, z, y, c).transpose(1, 0, 2).reshape(-1)
    valid = valid.astype(jnp.int32).transpose(1, 0, 2).reshape(-1)

    def swap(a):
        return shift(a, "c", 1)

    left, right = shift(hidden, "x", 1), shift(hidden, "x", -1)
    far_a, far_b = halves(left, right, w_own, places, valid)
    far_a, far_b = shift(far_a, "x", 1), shift(far_b, "x", -1)
    hiddens = (hidden, left, right, far_a, far_b)
    kv0, kv1 = project(at, hiddens, w_kv, cos, sin, 1, 2)

    around = [kv1] + [shift(kv1, "y", step) for step in (1, -1, 2)]
    plus, minus, line = kv0, kv0, [kv0]
    for k in range(3):
        plus, minus = shift(plus, "z", 1), shift(minus, "z", -1)
        if k == 0:
            minus = tie(minus, *around[1:])
        line += [plus, minus]
    line.append(shift(plus, "z", 1))
    [query] = project(at, hiddens, w_query, cos, tie(sin, kv0), w_query.shape[1] // BS, 1)
    w_all = lax.all_gather(tie(w_own, kv0, kv1), "x", axis=0, tiled=True)

    cat1 = lay(around, query)
    plus, minus, second = cat1, cat1, [cat1]
    for _ in range(3):
        plus, minus = shift(plus, "z", 1), shift(minus, "z", -1)
        second += [plus, minus]
    second.append(shift(plus, "z", 1))
    cat0 = lay(line)
    above, below = shift(cat0, "y", 1), shift(cat0, "y", -1)
    top, bottom = halves(above, below)
    first = [cat0, above, below, shift(top, "y", 1), shift(bottom, "y", -1)]

    arrays = first + second
    arrays += [swap(a) for a in arrays]
    pieces = [(a, 0, a.shape[0]) for a in arrays]
    own, ahead, across, behind = attend(order, places, valid, query, pieces)
    own = tie(own, w_all)
    context = jnp.concatenate(
        [own, shift(ahead, "x", 1), shift(behind, "x", -1), shift(across, "x", 2)], axis=1
    )
    mine, theirs = output(at // depth, context, swap(context), w_all)
    return join(jnp.reshape(c, (1,)).astype(jnp.int32), mine, swap(theirs))


def solution(mesh):
    fine = Mesh(mesh.devices.reshape(8, 4, 2, 4), ("z", "y", "c", "x"))
    ctx = ("z", "y", "c")
    placed = (
        P(ctx, "x"),
        P(None, "x"),
        P(None, "x"),
        P(None, "x"),
        P("x", None),
        P("x", None, None),
        P("x", None, None),
    )
    return jax.shard_map(
        body, mesh=fine, in_specs=placed, out_specs=P(ctx + ("x",), None), check_vma=False
    )
```

```python
import functools
import math

import jax
import jax.numpy as jnp
from jax import lax
from jax.experimental import pallas as pl
from jax.experimental.pallas import tpu as pltpu
from jax.sharding import Mesh, PartitionSpec as P

BS = 128
THETA = 10000000.0
F32 = jnp.float32
BF16 = jnp.bfloat16
MIB = 1 << 20
ANY = pl.BlockSpec(memory_space=pl.ANY)
VMEM = pl.BlockSpec(memory_space=pltpu.VMEM)
SMEM = pl.BlockSpec(memory_space=pltpu.SMEM)
HBM = pl.BlockSpec(memory_space=pltpu.HBM)


def shift(x, axis, step):
    n = lax.axis_size(axis)
    return lax.ppermute(x, axis, [(i, (i + step) % n) for i in range(n)])


def tie(x, *after):
    def kernel(*refs):
        pass

    return pl.pallas_call(
        kernel,
        out_shape=jax.ShapeDtypeStruct(x.shape, x.dtype),
        in_specs=[ANY] * (1 + len(after)),
        out_specs=ANY,
        input_output_aliases={0: 0},
        compiler_params=pltpu.CompilerParams(vmem_limit_bytes=MIB),
    )(x, *after)


def copy_rows(parts, outs, *after):
    arrays = [p[0] for p in parts]
    n = len(parts)

    def kernel(*refs):
        given, made, sem = refs[:n], refs[n + len(after) : -1], refs[-1]
        copies = []
        for k, (_, start, rows, to, row) in enumerate(parts):
            copies.append(
                pltpu.make_async_copy(
                    given[k].at[pl.ds(start, rows)], made[to].at[pl.ds(row, rows)], sem.at[k]
                )
            )
        for copy in copies:
            copy.start()
        for copy in copies:
            copy.wait()

    wide = arrays[0].shape[1]
    return pl.pallas_call(
        kernel,
        out_shape=[jax.ShapeDtypeStruct((r, wide), arrays[0].dtype) for r in outs],
        in_specs=[ANY] * (n + len(after)),
        out_specs=[ANY] * len(outs),
        scratch_shapes=[pltpu.SemaphoreType.DMA((n,))],
        compiler_params=pltpu.CompilerParams(vmem_limit_bytes=MIB),
        cost_estimate=pl.CostEstimate(
            flops=0, bytes_accessed=4 * wide * sum(p[2] for p in parts), transcendentals=0
        ),
    )(*arrays, *after)


def lay(arrays, *after):
    parts, row = [], 0
    for a in arrays:
        parts.append((a, 0, a.shape[0], 0, row))
        row += a.shape[0]
    return copy_rows(parts, [row], *after)[0]


def halves(a, b, *after):
    half = a.shape[0] // 2
    return copy_rows([(a, 0, half, 0, 0), (b, half, half, 1, 0)], [half, half], *after)


def project_kernel(
    roped, count, at_ref, own, left, right, far_a, far_b, w, cos, sin, *refs
):
    outs = refs[-count:]
    depth = own.shape[1]
    part_rows = own.shape[0] // count

    def rows(k):
        return w[pl.ds(pl.multiple_of(at_ref[k], 128), depth), :]

    total = jnp.dot(own[...], rows(0), preferred_element_type=F32)
    total += jnp.dot(left[...], rows(1), preferred_element_type=F32)
    total += jnp.dot(right[...], rows(2), preferred_element_type=F32)
    far = jnp.concatenate([far_a[...], far_b[...]], axis=0)
    total += jnp.dot(far, rows(3), preferred_element_type=F32)
    for head in range(total.shape[1] // BS):
        columns = slice(head * BS, (head + 1) * BS)
        part = total[:, columns]
        if head < roped:
            turned = jnp.concatenate([part[:, BS // 2 :], part[:, : BS // 2]], axis=1)
            part = part * cos[...] + turned * sin[...]
        part = part.astype(BF16)
        for k in range(count):
            outs[k][:, columns] = part[k * part_rows : (k + 1) * part_rows]


def project(at, pieces, w, cos, sin, roped, count, *after):
    rows = pieces[0].shape[0]
    return pl.pallas_call(
        functools.partial(project_kernel, roped, count),
        out_shape=[jax.ShapeDtypeStruct((rows // count, w.shape[1]), BF16)] * count,
        in_specs=[SMEM] + [VMEM] * 8 + [ANY] * len(after),
        out_specs=[VMEM] * count,
        compiler_params=pltpu.CompilerParams(vmem_limit_bytes=30 * MIB),
        cost_estimate=pl.CostEstimate(
            flops=2 * rows * w.shape[0] * w.shape[1],
            bytes_accessed=2 * (w.size + rows * w.shape[0] + rows * w.shape[1]),
            transcendentals=0,
        ),
    )(at, *pieces, w, cos, sin, *after)


def attend_kernel(count, heads, width, parts, at_ref, ok_ref, order_ref, q_ref, *refs):
    n = len(parts)
    arrays, outs, held, sem = refs[:n], refs[n : n + count], refs[n + count], refs[n + count + 1]
    copies, row = [], 0
    for k, (start, rows) in enumerate(parts):
        copies.append(
            pltpu.make_async_copy(
                arrays[k].at[pl.ds(start, rows)], held.at[pl.ds(row, rows)], sem.at[k]
            )
        )
        row += rows
    for copy in copies:
        copy.start()
    for copy in copies:
        copy.wait()
    scale = math.log2(math.e) / math.sqrt(BS)
    rows = lax.broadcasted_iota(jnp.int32, (BS, BS), 0)
    cols = lax.broadcasted_iota(jnp.int32, (BS, BS), 1)
    causal = cols <= rows
    for g in range(count):
        first = pl.multiple_of(order_ref[g] * BS, BS)
        for h in range(heads):
            base = (g * heads + h) * width
            query = q_ref[pl.ds(first, BS), h * BS : (h + 1) * BS]
            places = [pl.ds(pl.multiple_of(at_ref[base + s] * BS, BS), BS) for s in range(width)]
            keys = jnp.concatenate([held[place, :BS] for place in places], axis=0)
            values = jnp.concatenate([held[place, BS:] for place in places], axis=0)
            product = lax.dot_general(
                query, keys, (((1,), (1,)), ((), ())), preferred_element_type=F32
            )
            scores = []
            for s in range(width):
                keep = causal if s == 0 else ok_ref[base + s] > 0
                scores.append(jnp.where(keep, product[:, s * BS : (s + 1) * BS], -1e30))
            top = scores[0]
            for part in scores[1:]:
                top = jnp.maximum(top, part)
            top = jnp.max(top, axis=1, keepdims=True)
            raw = [jnp.exp2((part - top) * scale) for part in scores]
            total = raw[0]
            for part in raw[1:]:
                total = total + part
            total = jnp.sum(total, axis=1, keepdims=True)
            weights = jnp.concatenate([part.astype(BF16) for part in raw], axis=1)
            summed = jnp.dot(weights, values, preferred_element_type=F32)
            outs[g][:, h * BS : (h + 1) * BS] = (summed / total).astype(BF16)


def attend(order, at, ok, query, pieces):
    count, heads = order.shape[0], query.shape[1] // BS
    width = at.shape[0] // (count * heads)
    arrays = [p[0] for p in pieces]
    parts = tuple(p[1:] for p in pieces)
    length = sum(p[2] for p in pieces)
    wide = arrays[0].shape[1]
    return pl.pallas_call(
        functools.partial(attend_kernel, count, heads, width, parts),
        out_shape=[jax.ShapeDtypeStruct((BS, heads * BS), BF16)] * count,
        in_specs=[SMEM] * 3 + [VMEM] + [HBM] * len(arrays),
        out_specs=[VMEM] * count,
        scratch_shapes=[
            pltpu.VMEM((length, wide), BF16),
            pltpu.SemaphoreType.DMA((len(arrays),)),
        ],
        compiler_params=pltpu.CompilerParams(vmem_limit_bytes=60 * MIB),
        cost_estimate=pl.CostEstimate(
            flops=4 * count * heads * width * BS * BS * BS,
            bytes_accessed=2 * length * wide,
            transcendentals=count * heads * width * BS * BS,
        ),
    )(at, ok, order, query, *arrays)


def output_kernel(group_ref, mine, other, w, out_mine, out_other):
    both = jnp.concatenate([mine[...], other[...]], axis=0)
    count = group_ref.shape[0]
    deep = w.shape[0] // count
    total = None
    for k in range(count):
        rows = pl.ds(pl.multiple_of(group_ref[k] * deep, deep), deep)
        term = jnp.dot(
            both[:, k * deep : (k + 1) * deep], w[rows, :], preferred_element_type=F32
        )
        total = term if total is None else total + term
    total = total.astype(BF16)
    out_mine[...] = total[: mine.shape[0]]
    out_other[...] = total[mine.shape[0] :]


def output(groups, mine, other, w):
    rows, wide = mine.shape[0], w.shape[1]
    return pl.pallas_call(
        output_kernel,
        out_shape=[jax.ShapeDtypeStruct((rows, wide), BF16)] * 2,
        in_specs=[SMEM] + [VMEM] * 3,
        out_specs=[VMEM] * 2,
        compiler_params=pltpu.CompilerParams(vmem_limit_bytes=20 * MIB),
        cost_estimate=pl.CostEstimate(
            flops=4 * rows * w.size, bytes_accessed=2 * w.size, transcendentals=0
        ),
    )(groups, mine, other, w)


def join_kernel(core_ref, mine, theirs, out, sem):
    wide = mine.shape[1]
    first = pl.ds(pl.multiple_of(core_ref[0] * wide, BS), wide)
    second = pl.ds(pl.multiple_of((1 - core_ref[0]) * wide, BS), wide)
    copies = [
        pltpu.make_async_copy(mine, out.at[:, first], sem.at[0]),
        pltpu.make_async_copy(theirs, out.at[:, second], sem.at[1]),
    ]
    for copy in copies:
        copy.start()
    for copy in copies:
        copy.wait()


def join(core, mine, theirs):
    return pl.pallas_call(
        join_kernel,
        out_shape=jax.ShapeDtypeStruct((mine.shape[0], 2 * mine.shape[1]), BF16),
        in_specs=[SMEM, ANY, ANY],
        out_specs=ANY,
        scratch_shapes=[pltpu.SemaphoreType.DMA((2,))],
        compiler_params=pltpu.CompilerParams(vmem_limit_bytes=MIB),
    )(core, mine, theirs)


Z_ORDER = (0, 2, 4, 6, 7, 5, 3, 1)
Y_ORDER = (0, 2, 3, 1)


def slot_table(qblocks, columns, offsets):
    lead = columns.shape[:-1]
    count = qblocks.shape[0]
    diag = jnp.broadcast_to(qblocks[:, None], lead + (count, 1))
    back = qblocks[:, None] - offsets[..., None, :]
    upright = jnp.broadcast_to(columns[..., None, :], lead + (count, columns.shape[-1]))
    slots = jnp.concatenate([diag, back, upright], axis=-1)
    width = slots.shape[-1]
    same = slots[..., :, None] == slots[..., None, :]
    lower = jnp.tril(jnp.ones((width, width), dtype=bool), -1)
    repeated = jnp.any(same & lower, axis=-1)
    valid = (slots >= 0) & (slots <= qblocks[:, None]) & jnp.logical_not(repeated)
    return (jnp.maximum(slots, 0), valid)


def pick(table, index):
    out = jnp.full_like(index, table[0])
    for k in range(1, len(table)):
        out = jnp.where(index == k, table[k], out)
    return out


def place_of(block, z, y, c):
    owner, inner = block // 4, block % 4
    theirs_z, theirs_y, theirs_c = owner // 8, (owner // 2) % 4, owner % 2
    zo = pick(Z_ORDER, (theirs_z - z) % 8)
    yo = pick(Y_ORDER, (theirs_y - y) % 4)
    chunk = inner // 2
    pos = jnp.where(chunk == 0, yo * 8 + zo, zo * 4 + yo)
    swapped = (theirs_c != c).astype(jnp.int32)
    return ((swapped * 2 + chunk) * 32 + pos) * 2 + inner % 2


def body(hidden, w_query, w_key, w_value, w_output, vertical, slash_offsets):
    z, y, c, x = (lax.axis_index(a) for a in ("z", "y", "c", "x"))
    device = (z * 4 + y) * 2 + c
    tok_rows, depth = hidden.shape
    local = tok_rows // BS
    cut = w_output.shape[1] // 2

    half = BS // 2
    positions = device * tok_rows + jnp.arange(tok_rows, dtype=jnp.int32)
    freq = jnp.exp(-(jnp.arange(half, dtype=F32) * 2.0 / BS) * math.log(THETA))
    angle = positions.astype(F32)[:, None] * freq[None, :]
    cosine, sine = jnp.cos(angle), jnp.sin(angle)
    cos = jnp.concatenate([cosine, cosine], axis=1)
    sin = jnp.concatenate([-sine, sine], axis=1)
    w_kv = jnp.concatenate([w_key, w_value], axis=1)
    at = jnp.stack([x, (x + 3) % 4, (x + 1) % 4, (x + 2) % 4]).astype(jnp.int32) * depth
    w_own = lax.dynamic_slice_in_dim(w_output, c * cut, cut, axis=1)

    order = jnp.stack([(x + s) % 4 for s in range(local)]).astype(jnp.int32)
    slots, valid = slot_table(device * local + order, vertical[0], slash_offsets[0])
    places = place_of(slots, z, y, c).transpose(1, 0, 2).reshape(-1)
    valid = valid.astype(jnp.int32).transpose(1, 0, 2).reshape(-1)

    def swap(a):
        return shift(a, "c", 1)

    left, right = shift(hidden, "x", 1), shift(hidden, "x", -1)
    far_a, far_b = halves(left, right, w_own, places, valid)
    far_a, far_b = shift(far_a, "x", 1), shift(far_b, "x", -1)
    hiddens = (hidden, left, right, far_a, far_b)
    kv0, kv1 = project(at, hiddens, w_kv, cos, sin, 1, 2)

    around = [kv1] + [shift(kv1, "y", step) for step in (1, -1, 2)]
    plus, minus, line = kv0, kv0, [kv0]
    for k in range(3):
        plus, minus = shift(plus, "z", 1), shift(minus, "z", -1)
        if k == 0:
            minus = tie(minus, *around[1:])
        line += [plus, minus]
    line.append(shift(plus, "z", 1))
    [query] = project(at, hiddens, w_query, cos, tie(sin, kv0), w_query.shape[1] // BS, 1)
    w_all = lax.all_gather(tie(w_own, kv0, kv1), "x", axis=0, tiled=True)

    cat1 = lay(around)
    plus1, minus1 = shift(cat1, "z", 1), shift(cat1, "z", -1)
    cat0 = lay(line, query, plus1, minus1)
    above, below = shift(cat0, "y", 1), shift(cat0, "y", -1)
    plus2, minus2 = shift(plus1, "z", 1), shift(minus1, "z", -1)
    cat1 = tie(cat1, plus1, minus1)
    plus3, minus3 = shift(plus2, "z", 1), shift(minus2, "z", -1)
    far = shift(plus3, "z", 1)
    plus1, minus1 = tie(plus1, plus3), tie(minus1, plus3, minus2)
    plus2, minus2 = tie(plus2, plus3), tie(minus2, minus3)
    top, bottom = halves(above, below, plus3)
    cat0 = tie(cat0, above, below, plus3)
    above, below = tie(above, top), tie(below, bottom)
    first = [cat0, above, below, shift(top, "y", 1), shift(bottom, "y", -1)]
    second = [cat1, plus1, minus1, plus2, minus2, plus3, minus3, far]

    arrays = first + second
    arrays += [swap(a) for a in arrays]
    pieces = [(a, 0, a.shape[0]) for a in arrays]
    own, ahead, across, behind = attend(order, places, valid, query, pieces)
    own = tie(own, w_all)
    context = jnp.concatenate(
        [own, shift(ahead, "x", 1), shift(behind, "x", -1), shift(across, "x", 2)], axis=1
    )
    mine, theirs = output(at // depth, context, swap(context), w_all)
    return join(jnp.reshape(c, (1,)).astype(jnp.int32), mine, swap(theirs))


def solution(mesh):
    fine = Mesh(mesh.devices.reshape(8, 4, 2, 4), ("z", "y", "c", "x"))
    ctx = ("z", "y", "c")
    placed = (
        P(ctx, "x"),
        P(None, "x"),
        P(None, "x"),
        P(None, "x"),
        P("x", None),
        P("x", None, None),
        P("x", None, None),
    )
    return jax.shard_map(
        body, mesh=fine, in_specs=placed, out_specs=P(ctx + ("x",), None), check_vma=False
    )
```

```python
import functools
import math

import jax
import jax.numpy as jnp
from jax import lax
from jax.experimental import pallas as pl
from jax.experimental.pallas import tpu as pltpu
from jax.sharding import Mesh, PartitionSpec as P

BS = 128
THETA = 10000000.0
F32 = jnp.float32
BF16 = jnp.bfloat16
MIB = 1 << 20
ANY = pl.BlockSpec(memory_space=pl.ANY)
VMEM = pl.BlockSpec(memory_space=pltpu.VMEM)
SMEM = pl.BlockSpec(memory_space=pltpu.SMEM)
HBM = pl.BlockSpec(memory_space=pltpu.HBM)


def shift(x, axis, step):
    n = lax.axis_size(axis)
    return lax.ppermute(x, axis, [(i, (i + step) % n) for i in range(n)])


def tie(x, *after):
    def kernel(*refs):
        pass

    return pl.pallas_call(
        kernel,
        out_shape=jax.ShapeDtypeStruct(x.shape, x.dtype),
        in_specs=[ANY] * (1 + len(after)),
        out_specs=ANY,
        input_output_aliases={0: 0},
        compiler_params=pltpu.CompilerParams(vmem_limit_bytes=MIB),
    )(x, *after)


def copy_rows(parts, outs, *after):
    arrays = [p[0] for p in parts]
    n = len(parts)

    def kernel(*refs):
        given, made, sem = refs[:n], refs[n + len(after) : -1], refs[-1]
        copies = []
        for k, (_, start, rows, to, row) in enumerate(parts):
            copies.append(
                pltpu.make_async_copy(
                    given[k].at[pl.ds(start, rows)], made[to].at[pl.ds(row, rows)], sem.at[k]
                )
            )
        for copy in copies:
            copy.start()
        for copy in copies:
            copy.wait()

    wide = arrays[0].shape[1]
    return pl.pallas_call(
        kernel,
        out_shape=[jax.ShapeDtypeStruct((r, wide), arrays[0].dtype) for r in outs],
        in_specs=[ANY] * (n + len(after)),
        out_specs=[ANY] * len(outs),
        scratch_shapes=[pltpu.SemaphoreType.DMA((n,))],
        compiler_params=pltpu.CompilerParams(vmem_limit_bytes=MIB),
        cost_estimate=pl.CostEstimate(
            flops=0, bytes_accessed=4 * wide * sum(p[2] for p in parts), transcendentals=0
        ),
    )(*arrays, *after)


def lay(arrays, *after):
    parts, row = [], 0
    for a in arrays:
        parts.append((a, 0, a.shape[0], 0, row))
        row += a.shape[0]
    return copy_rows(parts, [row], *after)[0]


def halves(a, b, *after):
    half = a.shape[0] // 2
    return copy_rows([(a, 0, half, 0, 0), (b, half, half, 1, 0)], [half, half], *after)


def project_kernel(
    roped, count, at_ref, own, left, right, far_a, far_b, w, cos, sin, *refs
):
    outs = refs[-count:]
    depth = own.shape[1]
    part_rows = own.shape[0] // count

    def rows(k):
        return w[pl.ds(pl.multiple_of(at_ref[k], 128), depth), :]

    total = jnp.dot(own[...], rows(0), preferred_element_type=F32)
    total += jnp.dot(left[...], rows(1), preferred_element_type=F32)
    total += jnp.dot(right[...], rows(2), preferred_element_type=F32)
    far = jnp.concatenate([far_a[...], far_b[...]], axis=0)
    total += jnp.dot(far, rows(3), preferred_element_type=F32)
    for head in range(total.shape[1] // BS):
        columns = slice(head * BS, (head + 1) * BS)
        part = total[:, columns]
        if head < roped:
            turned = jnp.concatenate([part[:, BS // 2 :], part[:, : BS // 2]], axis=1)
            part = part * cos[...] + turned * sin[...]
        part = part.astype(BF16)
        for k in range(count):
            outs[k][:, columns] = part[k * part_rows : (k + 1) * part_rows]


def project(at, pieces, w, cos, sin, roped, count, *after):
    rows = pieces[0].shape[0]
    return pl.pallas_call(
        functools.partial(project_kernel, roped, count),
        out_shape=[jax.ShapeDtypeStruct((rows // count, w.shape[1]), BF16)] * count,
        in_specs=[SMEM] + [VMEM] * 8 + [ANY] * len(after),
        out_specs=[VMEM] * count,
        compiler_params=pltpu.CompilerParams(vmem_limit_bytes=30 * MIB),
        cost_estimate=pl.CostEstimate(
            flops=2 * rows * w.shape[0] * w.shape[1],
            bytes_accessed=2 * (w.size + rows * w.shape[0] + rows * w.shape[1]),
            transcendentals=0,
        ),
    )(at, *pieces, w, cos, sin, *after)


def attend_kernel(count, heads, width, parts, at_ref, ok_ref, order_ref, q_ref, *refs):
    n = len(parts)
    arrays, outs, held, sem = refs[:n], refs[n : n + count], refs[n + count], refs[n + count + 1]
    copies, row = [], 0
    for k, (start, rows) in enumerate(parts):
        copies.append(
            pltpu.make_async_copy(
                arrays[k].at[pl.ds(start, rows)], held.at[pl.ds(row, rows)], sem.at[k]
            )
        )
        row += rows
    for copy in copies:
        copy.start()
    for copy in copies:
        copy.wait()
    scale = math.log2(math.e) / math.sqrt(BS)
    rows = lax.broadcasted_iota(jnp.int32, (BS, BS), 0)
    cols = lax.broadcasted_iota(jnp.int32, (BS, BS), 1)
    causal = cols <= rows
    for g in range(count):
        first = pl.multiple_of(order_ref[g] * BS, BS)
        for h in range(heads):
            base = (g * heads + h) * width
            query = q_ref[pl.ds(first, BS), h * BS : (h + 1) * BS]
            places = [pl.ds(pl.multiple_of(at_ref[base + s] * BS, BS), BS) for s in range(width)]
            keys = jnp.concatenate([held[place, :BS] for place in places], axis=0)
            values = jnp.concatenate([held[place, BS:] for place in places], axis=0)
            product = lax.dot_general(
                query, keys, (((1,), (1,)), ((), ())), preferred_element_type=F32
            )
            scores = []
            for s in range(width):
                keep = causal if s == 0 else ok_ref[base + s] > 0
                scores.append(jnp.where(keep, product[:, s * BS : (s + 1) * BS], -1e30))
            top = scores[0]
            for part in scores[1:]:
                top = jnp.maximum(top, part)
            top = jnp.max(top, axis=1, keepdims=True)
            raw = [jnp.exp2((part - top) * scale) for part in scores]
            total = raw[0]
            for part in raw[1:]:
                total = total + part
            total = jnp.sum(total, axis=1, keepdims=True)
            weights = jnp.concatenate([part.astype(BF16) for part in raw], axis=1)
            summed = jnp.dot(weights, values, preferred_element_type=F32)
            outs[g][:, h * BS : (h + 1) * BS] = (summed / total).astype(BF16)


def attend(order, at, ok, query, pieces):
    count, heads = order.shape[0], query.shape[1] // BS
    width = at.shape[0] // (count * heads)
    arrays = [p[0] for p in pieces]
    parts = tuple(p[1:] for p in pieces)
    length = sum(p[2] for p in pieces)
    wide = arrays[0].shape[1]
    return pl.pallas_call(
        functools.partial(attend_kernel, count, heads, width, parts),
        out_shape=[jax.ShapeDtypeStruct((BS, heads * BS), BF16)] * count,
        in_specs=[SMEM] * 3 + [VMEM] + [HBM] * len(arrays),
        out_specs=[VMEM] * count,
        scratch_shapes=[
            pltpu.VMEM((length, wide), BF16),
            pltpu.SemaphoreType.DMA((len(arrays),)),
        ],
        compiler_params=pltpu.CompilerParams(vmem_limit_bytes=60 * MIB),
        cost_estimate=pl.CostEstimate(
            flops=4 * count * heads * width * BS * BS * BS,
            bytes_accessed=2 * length * wide,
            transcendentals=count * heads * width * BS * BS,
        ),
    )(at, ok, order, query, *arrays)


def output_kernel(group_ref, mine, other, w, out_mine, out_other):
    both = jnp.concatenate([mine[...], other[...]], axis=0)
    count = group_ref.shape[0]
    deep = w.shape[0] // count
    total = None
    for k in range(count):
        rows = pl.ds(pl.multiple_of(group_ref[k] * deep, deep), deep)
        term = jnp.dot(
            both[:, k * deep : (k + 1) * deep], w[rows, :], preferred_element_type=F32
        )
        total = term if total is None else total + term
    total = total.astype(BF16)
    out_mine[...] = total[: mine.shape[0]]
    out_other[...] = total[mine.shape[0] :]


def output(groups, mine, other, w):
    rows, wide = mine.shape[0], w.shape[1]
    return pl.pallas_call(
        output_kernel,
        out_shape=[jax.ShapeDtypeStruct((rows, wide), BF16)] * 2,
        in_specs=[SMEM] + [VMEM] * 3,
        out_specs=[VMEM] * 2,
        compiler_params=pltpu.CompilerParams(vmem_limit_bytes=20 * MIB),
        cost_estimate=pl.CostEstimate(
            flops=4 * rows * w.size, bytes_accessed=2 * w.size, transcendentals=0
        ),
    )(groups, mine, other, w)


def join_kernel(core_ref, mine, theirs, out, sem):
    wide = mine.shape[1]
    first = pl.ds(pl.multiple_of(core_ref[0] * wide, BS), wide)
    second = pl.ds(pl.multiple_of((1 - core_ref[0]) * wide, BS), wide)
    copies = [
        pltpu.make_async_copy(mine, out.at[:, first], sem.at[0]),
        pltpu.make_async_copy(theirs, out.at[:, second], sem.at[1]),
    ]
    for copy in copies:
        copy.start()
    for copy in copies:
        copy.wait()


def join(core, mine, theirs):
    return pl.pallas_call(
        join_kernel,
        out_shape=jax.ShapeDtypeStruct((mine.shape[0], 2 * mine.shape[1]), BF16),
        in_specs=[SMEM, ANY, ANY],
        out_specs=ANY,
        scratch_shapes=[pltpu.SemaphoreType.DMA((2,))],
        compiler_params=pltpu.CompilerParams(vmem_limit_bytes=MIB),
    )(core, mine, theirs)


Z_ORDER = (0, 2, 4, 6, 7, 5, 3, 1)
Y_ORDER = (0, 2, 3, 1)


def slot_table(qblocks, columns, offsets):
    lead = columns.shape[:-1]
    count = qblocks.shape[0]
    diag = jnp.broadcast_to(qblocks[:, None], lead + (count, 1))
    back = qblocks[:, None] - offsets[..., None, :]
    upright = jnp.broadcast_to(columns[..., None, :], lead + (count, columns.shape[-1]))
    slots = jnp.concatenate([diag, back, upright], axis=-1)
    width = slots.shape[-1]
    same = slots[..., :, None] == slots[..., None, :]
    lower = jnp.tril(jnp.ones((width, width), dtype=bool), -1)
    repeated = jnp.any(same & lower, axis=-1)
    valid = (slots >= 0) & (slots <= qblocks[:, None]) & jnp.logical_not(repeated)
    return (jnp.maximum(slots, 0), valid)


def pick(table, index):
    out = jnp.full_like(index, table[0])
    for k in range(1, len(table)):
        out = jnp.where(index == k, table[k], out)
    return out


def place_of(block, z, y, c):
    owner, inner = block // 4, block % 4
    theirs_z, theirs_y, theirs_c = owner // 8, (owner // 2) % 4, owner % 2
    zo = pick(Z_ORDER, (theirs_z - z) % 8)
    yo = pick(Y_ORDER, (theirs_y - y) % 4)
    chunk = inner // 2
    pos = jnp.where(chunk == 0, yo * 8 + zo, zo * 4 + yo)
    swapped = (theirs_c != c).astype(jnp.int32)
    return ((swapped * 2 + chunk) * 32 + pos) * 2 + inner % 2


def body(hidden, w_query, w_key, w_value, w_output, vertical, slash_offsets):
    z, y, c, x = (lax.axis_index(a) for a in ("z", "y", "c", "x"))
    device = (z * 4 + y) * 2 + c
    tok_rows, depth = hidden.shape
    local = tok_rows // BS
    cut = w_output.shape[1] // 2

    half = BS // 2
    positions = device * tok_rows + jnp.arange(tok_rows, dtype=jnp.int32)
    freq = jnp.exp(-(jnp.arange(half, dtype=F32) * 2.0 / BS) * math.log(THETA))
    angle = positions.astype(F32)[:, None] * freq[None, :]
    cosine, sine = jnp.cos(angle), jnp.sin(angle)
    cos = jnp.concatenate([cosine, cosine], axis=1)
    sin = jnp.concatenate([-sine, sine], axis=1)
    w_kv = jnp.concatenate([w_key, w_value], axis=1)
    at = jnp.stack([x, (x + 3) % 4, (x + 1) % 4, (x + 2) % 4]).astype(jnp.int32) * depth
    w_own = lax.dynamic_slice_in_dim(w_output, c * cut, cut, axis=1)

    order = jnp.stack([(x + s) % 4 for s in range(local)]).astype(jnp.int32)
    slots, valid = slot_table(device * local + order, vertical[0], slash_offsets[0])
    places = place_of(slots, z, y, c).transpose(1, 0, 2).reshape(-1)
    valid = valid.astype(jnp.int32).transpose(1, 0, 2).reshape(-1)

    def swap(a):
        return shift(a, "c", 1)

    left, right = shift(hidden, "x", 1), shift(hidden, "x", -1)
    far_a, far_b = halves(left, right, w_own, places, valid)
    far_a, far_b = shift(far_a, "x", 1), shift(far_b, "x", -1)
    hiddens = (hidden, left, right, far_a, far_b)
    kv0, kv1 = project(at, hiddens, w_kv, cos, sin, 1, 2)

    around = [kv1] + [shift(kv1, "y", step) for step in (1, -1, 2)]
    plus, minus, line = kv0, kv0, [kv0]
    for k in range(3):
        plus, minus = shift(plus, "z", 1), shift(minus, "z", -1)
        if k == 0:
            minus = tie(minus, *around[1:])
        line += [plus, minus]
    line.append(shift(minus, "z", -1))
    [query] = project(at, hiddens, w_query, cos, tie(sin, kv0), w_query.shape[1] // BS, 1)
    w_all = lax.all_gather(tie(w_own, kv0, kv1), "x", axis=0, tiled=True)

    cat1 = lay(around, line[5], line[6])
    plus1, minus1 = shift(cat1, "z", 1), shift(cat1, "z", -1)
    cat0 = lay(line)
    above, below = shift(cat0, "y", 1), shift(cat0, "y", -1)
    plus2, minus2 = shift(plus1, "z", 1), shift(minus1, "z", -1)
    cat1 = tie(cat1, plus1, minus1)
    plus3, minus3 = shift(plus2, "z", 1), shift(minus2, "z", -1)
    far = shift(plus3, "z", 1)
    plus1, minus1 = tie(plus1, plus3), tie(minus1, plus3, minus2)
    plus2, minus2 = tie(plus2, plus3), tie(minus2, minus3)
    top, bottom = halves(above, below, plus3, query)
    cat0 = tie(cat0, above, below, plus3)
    above, below = tie(above, top), tie(below, bottom)
    first = [cat0, above, below, shift(top, "y", 1), shift(bottom, "y", -1)]
    second = [cat1, plus1, minus1, plus2, minus2, plus3, minus3, far]

    arrays = first + second
    arrays += [swap(a) for a in arrays]
    pieces = [(a, 0, a.shape[0]) for a in arrays]
    own, ahead, across, behind = attend(order, places, valid, query, pieces)
    own = tie(own, w_all)
    context = jnp.concatenate(
        [own, shift(ahead, "x", 1), shift(behind, "x", -1), shift(across, "x", 2)], axis=1
    )
    mine, theirs = output(at // depth, context, swap(context), w_all)
    return join(jnp.reshape(c, (1,)).astype(jnp.int32), mine, swap(theirs))


def solution(mesh):
    fine = Mesh(mesh.devices.reshape(8, 4, 2, 4), ("z", "y", "c", "x"))
    ctx = ("z", "y", "c")
    placed = (
        P(ctx, "x"),
        P(None, "x"),
        P(None, "x"),
        P(None, "x"),
        P("x", None),
        P("x", None, None),
        P("x", None, None),
    )
    return jax.shard_map(
        body, mesh=fine, in_specs=placed, out_specs=P(ctx + ("x",), None), check_vma=False
    )
```

```python
import functools
import math

import jax
import jax.numpy as jnp
from jax import lax
from jax.experimental import pallas as pl
from jax.experimental.pallas import tpu as pltpu
from jax.sharding import Mesh, PartitionSpec as P

BS = 128
THETA = 10000000.0
F32 = jnp.float32
BF16 = jnp.bfloat16
MIB = 1 << 20
ANY = pl.BlockSpec(memory_space=pl.ANY)
VMEM = pl.BlockSpec(memory_space=pltpu.VMEM)
SMEM = pl.BlockSpec(memory_space=pltpu.SMEM)
HBM = pl.BlockSpec(memory_space=pltpu.HBM)


def shift(x, axis, step):
    n = lax.axis_size(axis)
    return lax.ppermute(x, axis, [(i, (i + step) % n) for i in range(n)])


def tie(x, *after):
    def kernel(*refs):
        pass

    return pl.pallas_call(
        kernel,
        out_shape=jax.ShapeDtypeStruct(x.shape, x.dtype),
        in_specs=[ANY] * (1 + len(after)),
        out_specs=ANY,
        input_output_aliases={0: 0},
        compiler_params=pltpu.CompilerParams(vmem_limit_bytes=MIB),
    )(x, *after)


def copy_rows(parts, outs, *after):
    arrays = [p[0] for p in parts]
    n = len(parts)

    def kernel(*refs):
        given, made, sem = refs[:n], refs[n + len(after) : -1], refs[-1]
        copies = []
        for k, (_, start, rows, to, row) in enumerate(parts):
            copies.append(
                pltpu.make_async_copy(
                    given[k].at[pl.ds(start, rows)], made[to].at[pl.ds(row, rows)], sem.at[k]
                )
            )
        for copy in copies:
            copy.start()
        for copy in copies:
            copy.wait()

    wide = arrays[0].shape[1]
    return pl.pallas_call(
        kernel,
        out_shape=[jax.ShapeDtypeStruct((r, wide), arrays[0].dtype) for r in outs],
        in_specs=[ANY] * (n + len(after)),
        out_specs=[ANY] * len(outs),
        scratch_shapes=[pltpu.SemaphoreType.DMA((n,))],
        compiler_params=pltpu.CompilerParams(vmem_limit_bytes=MIB),
        cost_estimate=pl.CostEstimate(
            flops=0, bytes_accessed=4 * wide * sum(p[2] for p in parts), transcendentals=0
        ),
    )(*arrays, *after)


def lay(arrays, *after):
    parts, row = [], 0
    for a in arrays:
        parts.append((a, 0, a.shape[0], 0, row))
        row += a.shape[0]
    return copy_rows(parts, [row], *after)[0]


def halves(a, b, *after):
    half = a.shape[0] // 2
    return copy_rows([(a, 0, half, 0, 0), (b, half, half, 1, 0)], [half, half], *after)


def project_kernel(
    roped, count, at_ref, own, left, right, far_a, far_b, w, cos, sin, *refs
):
    outs = refs[-count:]
    depth = own.shape[1]
    part_rows = own.shape[0] // count

    def rows(k):
        return w[pl.ds(pl.multiple_of(at_ref[k], 128), depth), :]

    total = jnp.dot(own[...], rows(0), preferred_element_type=F32)
    total += jnp.dot(left[...], rows(1), preferred_element_type=F32)
    total += jnp.dot(right[...], rows(2), preferred_element_type=F32)
    far = jnp.concatenate([far_a[...], far_b[...]], axis=0)
    total += jnp.dot(far, rows(3), preferred_element_type=F32)
    for head in range(total.shape[1] // BS):
        columns = slice(head * BS, (head + 1) * BS)
        part = total[:, columns]
        if head < roped:
            turned = jnp.concatenate([part[:, BS // 2 :], part[:, : BS // 2]], axis=1)
            part = part * cos[...] + turned * sin[...]
        part = part.astype(BF16)
        for k in range(count):
            outs[k][:, columns] = part[k * part_rows : (k + 1) * part_rows]


def project(at, pieces, w, cos, sin, roped, count, *after):
    rows = pieces[0].shape[0]
    return pl.pallas_call(
        functools.partial(project_kernel, roped, count),
        out_shape=[jax.ShapeDtypeStruct((rows // count, w.shape[1]), BF16)] * count,
        in_specs=[SMEM] + [VMEM] * 8 + [ANY] * len(after),
        out_specs=[VMEM] * count,
        compiler_params=pltpu.CompilerParams(vmem_limit_bytes=30 * MIB),
        cost_estimate=pl.CostEstimate(
            flops=2 * rows * w.shape[0] * w.shape[1],
            bytes_accessed=2 * (w.size + rows * w.shape[0] + rows * w.shape[1]),
            transcendentals=0,
        ),
    )(at, *pieces, w, cos, sin, *after)


def attend_kernel(count, heads, width, parts, at_ref, ok_ref, order_ref, q_ref, *refs):
    n = len(parts)
    arrays, outs, held, sem = refs[:n], refs[n : n + count], refs[n + count], refs[n + count + 1]
    copies, row = [], 0
    for k, (start, rows) in enumerate(parts):
        copies.append(
            pltpu.make_async_copy(
                arrays[k].at[pl.ds(start, rows)], held.at[pl.ds(row, rows)], sem.at[k]
            )
        )
        row += rows
    for copy in copies:
        copy.start()
    for copy in copies:
        copy.wait()
    scale = math.log2(math.e) / math.sqrt(BS)
    rows = lax.broadcasted_iota(jnp.int32, (BS, BS), 0)
    cols = lax.broadcasted_iota(jnp.int32, (BS, BS), 1)
    causal = cols <= rows
    for g in range(count):
        first = pl.multiple_of(order_ref[g] * BS, BS)
        for h in range(heads):
            base = (g * heads + h) * width
            query = q_ref[pl.ds(first, BS), h * BS : (h + 1) * BS]
            places = [pl.ds(pl.multiple_of(at_ref[base + s] * BS, BS), BS) for s in range(width)]
            keys = jnp.concatenate([held[place, :BS] for place in places], axis=0)
            values = jnp.concatenate([held[place, BS:] for place in places], axis=0)
            product = lax.dot_general(
                query, keys, (((1,), (1,)), ((), ())), preferred_element_type=F32
            )
            scores = []
            for s in range(width):
                keep = causal if s == 0 else ok_ref[base + s] > 0
                scores.append(jnp.where(keep, product[:, s * BS : (s + 1) * BS], -1e30))
            top = scores[0]
            for part in scores[1:]:
                top = jnp.maximum(top, part)
            top = jnp.max(top, axis=1, keepdims=True)
            raw = [jnp.exp2((part - top) * scale) for part in scores]
            total = raw[0]
            for part in raw[1:]:
                total = total + part
            total = jnp.sum(total, axis=1, keepdims=True)
            weights = jnp.concatenate([part.astype(BF16) for part in raw], axis=1)
            summed = jnp.dot(weights, values, preferred_element_type=F32)
            outs[g][:, h * BS : (h + 1) * BS] = (summed / total).astype(BF16)


def attend(order, at, ok, query, pieces):
    count, heads = order.shape[0], query.shape[1] // BS
    width = at.shape[0] // (count * heads)
    arrays = [p[0] for p in pieces]
    parts = tuple(p[1:] for p in pieces)
    length = sum(p[2] for p in pieces)
    wide = arrays[0].shape[1]
    return pl.pallas_call(
        functools.partial(attend_kernel, count, heads, width, parts),
        out_shape=[jax.ShapeDtypeStruct((BS, heads * BS), BF16)] * count,
        in_specs=[SMEM] * 3 + [VMEM] + [HBM] * len(arrays),
        out_specs=[VMEM] * count,
        scratch_shapes=[
            pltpu.VMEM((length, wide), BF16),
            pltpu.SemaphoreType.DMA((len(arrays),)),
        ],
        compiler_params=pltpu.CompilerParams(vmem_limit_bytes=60 * MIB),
        cost_estimate=pl.CostEstimate(
            flops=4 * count * heads * width * BS * BS * BS,
            bytes_accessed=2 * length * wide,
            transcendentals=count * heads * width * BS * BS,
        ),
    )(at, ok, order, query, *arrays)


def output_kernel(mine, other, *refs):
    out_mine, out_other = refs[-2:]
    both = jnp.concatenate([mine[...], other[...]], axis=0)
    total, row = None, 0
    for w in refs[:-2]:
        part = both[:, row : row + w.shape[0]]
        term = jnp.dot(part, w[...], preferred_element_type=F32)
        total = term if total is None else total + term
        row += w.shape[0]
    total = total.astype(BF16)
    out_mine[...] = total[: mine.shape[0]]
    out_other[...] = total[mine.shape[0] :]


def output(mine, other, weights):
    rows, wide = mine.shape[0], weights[0].shape[1]
    size = sum(w.shape[0] for w in weights) * wide
    return pl.pallas_call(
        output_kernel,
        out_shape=[jax.ShapeDtypeStruct((rows, wide), BF16)] * 2,
        in_specs=[VMEM] * (2 + len(weights)),
        out_specs=[VMEM] * 2,
        compiler_params=pltpu.CompilerParams(vmem_limit_bytes=20 * MIB),
        cost_estimate=pl.CostEstimate(
            flops=4 * rows * size, bytes_accessed=2 * size, transcendentals=0
        ),
    )(mine, other, *weights)


def join_kernel(core_ref, mine, theirs, out, sem):
    wide = mine.shape[1]
    first = pl.ds(pl.multiple_of(core_ref[0] * wide, BS), wide)
    second = pl.ds(pl.multiple_of((1 - core_ref[0]) * wide, BS), wide)
    copies = [
        pltpu.make_async_copy(mine, out.at[:, first], sem.at[0]),
        pltpu.make_async_copy(theirs, out.at[:, second], sem.at[1]),
    ]
    for copy in copies:
        copy.start()
    for copy in copies:
        copy.wait()


def join(core, mine, theirs):
    return pl.pallas_call(
        join_kernel,
        out_shape=jax.ShapeDtypeStruct((mine.shape[0], 2 * mine.shape[1]), BF16),
        in_specs=[SMEM, ANY, ANY],
        out_specs=ANY,
        scratch_shapes=[pltpu.SemaphoreType.DMA((2,))],
        compiler_params=pltpu.CompilerParams(vmem_limit_bytes=MIB),
    )(core, mine, theirs)


Z_ORDER = (0, 2, 4, 6, 7, 5, 3, 1)
Y_ORDER = (0, 2, 3, 1)


def slot_table(qblocks, columns, offsets):
    lead = columns.shape[:-1]
    count = qblocks.shape[0]
    diag = jnp.broadcast_to(qblocks[:, None], lead + (count, 1))
    back = qblocks[:, None] - offsets[..., None, :]
    upright = jnp.broadcast_to(columns[..., None, :], lead + (count, columns.shape[-1]))
    slots = jnp.concatenate([diag, back, upright], axis=-1)
    width = slots.shape[-1]
    same = slots[..., :, None] == slots[..., None, :]
    lower = jnp.tril(jnp.ones((width, width), dtype=bool), -1)
    repeated = jnp.any(same & lower, axis=-1)
    valid = (slots >= 0) & (slots <= qblocks[:, None]) & jnp.logical_not(repeated)
    return (jnp.maximum(slots, 0), valid)


def pick(table, index):
    out = jnp.full_like(index, table[0])
    for k in range(1, len(table)):
        out = jnp.where(index == k, table[k], out)
    return out


def place_of(block, z, y, c):
    owner, inner = block // 4, block % 4
    theirs_z, theirs_y, theirs_c = owner // 8, (owner // 2) % 4, owner % 2
    zo = pick(Z_ORDER, (theirs_z - z) % 8)
    yo = pick(Y_ORDER, (theirs_y - y) % 4)
    chunk = inner // 2
    pos = jnp.where(chunk == 0, yo * 8 + zo, zo * 4 + yo)
    swapped = (theirs_c != c).astype(jnp.int32)
    return ((swapped * 2 + chunk) * 32 + pos) * 2 + inner % 2


def body(hidden, w_query, w_key, w_value, w_output, vertical, slash_offsets):
    z, y, c, x = (lax.axis_index(a) for a in ("z", "y", "c", "x"))
    device = (z * 4 + y) * 2 + c
    tok_rows, depth = hidden.shape
    local = tok_rows // BS
    cut = w_output.shape[1] // 2

    half = BS // 2
    positions = device * tok_rows + jnp.arange(tok_rows, dtype=jnp.int32)
    freq = jnp.exp(-(jnp.arange(half, dtype=F32) * 2.0 / BS) * math.log(THETA))
    angle = positions.astype(F32)[:, None] * freq[None, :]
    cosine, sine = jnp.cos(angle), jnp.sin(angle)
    cos = jnp.concatenate([cosine, cosine], axis=1)
    sin = jnp.concatenate([-sine, sine], axis=1)
    w_kv = jnp.concatenate([w_key, w_value], axis=1)
    at = jnp.stack([x, (x + 3) % 4, (x + 1) % 4, (x + 2) % 4]).astype(jnp.int32) * depth
    mid = w_output.shape[0] // 2
    w_a, w_b = (lax.dynamic_slice(w_output, (k * mid, c * cut), (mid, cut)) for k in range(2))

    order = jnp.stack([(x + s) % 4 for s in range(local)]).astype(jnp.int32)
    slots, valid = slot_table(device * local + order, vertical[0], slash_offsets[0])
    places = place_of(slots, z, y, c).transpose(1, 0, 2).reshape(-1)
    valid = valid.astype(jnp.int32).transpose(1, 0, 2).reshape(-1)

    def swap(a):
        return shift(a, "c", 1)

    left, right = shift(hidden, "x", 1), shift(hidden, "x", -1)
    far_a, far_b = halves(left, right, w_a, w_b, places, valid)
    far_a, far_b = shift(far_a, "x", 1), shift(far_b, "x", -1)
    hiddens = (hidden, left, right, far_a, far_b)
    kv0, kv1 = project(at, hiddens, w_kv, cos, sin, 1, 2)

    around = [kv1] + [shift(kv1, "y", step) for step in (1, -1, 2)]
    plus, minus, line = kv0, kv0, [kv0]
    for k in range(3):
        plus, minus = shift(plus, "z", 1), shift(minus, "z", -1)
        if k == 0:
            minus = tie(minus, *around[1:])
        line += [plus, minus]
    line.append(shift(minus, "z", -1))
    [query] = project(at, hiddens, w_query, cos, tie(sin, kv0), w_query.shape[1] // BS, 1)
    w_a, w_b = tie(w_a, around[3]), tie(w_b, around[3])
    left_a, right_b = shift(w_a, "x", 1), shift(w_b, "x", -1)

    cat1 = lay(around, *line[5:], left_a, right_b)
    plus1, minus1 = shift(cat1, "z", 1), shift(cat1, "z", -1)
    cat0 = lay(line)
    w_b = tie(w_b, left_a, right_b)
    left_b = shift(w_b, "x", 1)
    above, below = shift(cat0, "y", 1), shift(cat0, "y", -1)
    plus2, minus2 = shift(plus1, "z", 1), shift(minus1, "z", -1)
    cat1 = tie(cat1, plus1, minus1)
    plus3, minus3 = shift(plus2, "z", 1), shift(minus2, "z", -1)
    far = shift(plus3, "z", 1)
    plus1, minus1 = tie(plus1, plus3), tie(minus1, plus3, minus2)
    plus2, minus2 = tie(plus2, plus3), tie(minus2, minus3)
    top, bottom = halves(above, below, plus3, query, left_b)
    w_a = tie(w_a, left_b)
    right_a = shift(w_a, "x", -1)
    cat0 = tie(cat0, above, below, plus3)
    above, below = tie(above, top), tie(below, bottom)
    first = [cat0, above, below, shift(top, "y", 1), shift(bottom, "y", -1)]
    second = [cat1, plus1, minus1, plus2, minus2, plus3, minus3, far]

    arrays = first + second
    arrays += [swap(a) for a in arrays]
    pieces = [(a, 0, a.shape[0]) for a in arrays]
    far_a, far_b = shift(left_a, "x", 1), shift(right_b, "x", -1)
    query = tie(query, right_a, far_a, far_b)
    own, ahead, across, behind = attend(order, places, valid, query, pieces)
    context = jnp.concatenate(
        [own, shift(ahead, "x", 1), shift(behind, "x", -1), shift(across, "x", 2)], axis=1
    )
    weights = (w_a, w_b, left_a, left_b, right_a, right_b, far_a, far_b)
    mine, theirs = output(context, swap(context), weights)
    return join(jnp.reshape(c, (1,)).astype(jnp.int32), mine, swap(theirs))


def solution(mesh):
    fine = Mesh(mesh.devices.reshape(8, 4, 2, 4), ("z", "y", "c", "x"))
    ctx = ("z", "y", "c")
    placed = (
        P(ctx, "x"),
        P(None, "x"),
        P(None, "x"),
        P(None, "x"),
        P("x", None),
        P("x", None, None),
        P("x", None, None),
    )
    return jax.shard_map(
        body, mesh=fine, in_specs=placed, out_specs=P(ctx + ("x",), None), check_vma=False
    )
```
